512 devices in a mesh: member: 4 (over x_lo, core), gx: 16 (over x_hi, y), gy: 8 (over z).
Axes of the slice: x: 4 (x_hi: 2, x_lo: 2; x = x_hi * 2 + x_lo), y: 8, z: 8, core: 2. Of those that a mesh axis runs over, the one named last changes fastest.
Arguments:
- forcing: float32 [4, 2, 512, 1024], P('member', None, 'gx', 'gy'), may hold values from -6 to 6
- strength: float32 [64, 128], P('gx', 'gy'), may hold values from 0.3 to 2
- mask: int32 [512, 1024], P('gx', 'gy'), may hold values 0 or 1
- send_cell: int32 [4, 16, 8, 4096], P('member', 'gx', 'gy'), may hold values from 0 to 4095, as said below
- send_code: int32 [4, 16, 8, 4096], P('member', 'gx', 'gy'), may hold values from 0 to 16
- recv_buoy: int32 [4, 16, 8, 4096], P('member', 'gx', 'gy'), may hold values from 0 to 255
- observed: float32 [4, 16, 8, 2, 256], P('member', 'gx', 'gy'), may hold values from -6 to 6
Outputs:
- misfit: float32 [4, 16, 8, 2, 256], P('member', 'gx', 'gy')
- gradient: float32 [64, 128], P('gx', 'gy')
The draws below stay inside these ranges and needn't reach their ends.
Inputs may be any that keep to these rules, and one draw needn't show every extreme that they name: `send_cell`: a cell index of the sending device's 32 x 128 tile, row-major.
All inputs are finite; a program needn't handle non-finite values. No bound on the sum of `mask` on one device may be relied on, other than what follows from the above.
Results may differ from the reference program's by a relative error of at most 0.0001.
Values sent between devices are 32-bit elements; how exact they have to be, the bound alone decides.
No kernel may reach another device: no remote copies, remote signals or barrier semaphores. Data moves between devices by JAX's collectives and lax.ppermute only.
A program may use at most 64 MiB of HBM per device.

```python
import math
import jax
import jax.numpy as jnp

CX = 32
CY = 128
SUBCYCLES = 8
CAP = 512
BUOYS = 256
MEMBERS = 4
ENTRIES = 4096
NX = 512
NY = 1024
N_GX = 16
N_GY = 8


def draw_send_cell(key, part):
    key = jax.random.fold_in(key, 11)
    shape = (MEMBERS, NX // CX, NY // CY, ENTRIES)
    keys = jax.random.split(key, 5)
    choose = jax.random.randint(keys[0], shape, 0, 8)
    side = jax.random.randint(keys[1], shape, 0, 4)
    along_y = jax.random.randint(keys[2], shape, 0, CY)
    along_x = jax.random.randint(keys[3], shape, 0, CX)
    row = jnp.where(side == 0, 0, jnp.where(side == 1, CX - 1, along_x))
    col = jnp.where(side == 2, 0, jnp.where(side == 3, CY - 1, along_y))
    edge_cell = row * CY + col
    anywhere = jax.random.randint(keys[4], shape, 0, CX * CY)
    cell = jnp.where(choose < 6, edge_cell, anywhere)
    cell = cell.at[0, 0, 0, 0].set(0)
    cell = cell.at[0, 0, 0, 1].set(CX * CY - 1)
    return cell.astype(jnp.int32)


def with_ends(result, own_key, smallest, top_value):
    longest = result.shape.index(max(result.shape))
    spots = []
    for shift in (0, 1):
        where = [jax.random.randint(jax.random.fold_in(own_key, axis), (), 0, length) for axis, length in enumerate(result.shape)]
        where[longest] = (where[longest] + shift) % result.shape[longest]
        spots.append(tuple(where))
    return result.at[spots[0]].set(smallest).at[spots[1]].set(top_value)


def levels(own_key, shape, cuts, low, high):
    loudness, own = 1.0, jax.random.fold_in(own_key, 6)
    for dim, shards_of in cuts:
        heights = jnp.exp(jax.random.uniform(jax.random.fold_in(own, dim), (shards_of,), jnp.float32, low / len(cuts), high / len(cuts)))
        loudness = loudness * jnp.repeat(heights, shape[dim] // shards_of).reshape([-1 if axis == dim else 1 for axis in range(len(shape))])
    return loudness


def bell_draw(stream_key, extent, scale, most, pieces=(), kind=jnp.bfloat16):
    factor_of = levels(stream_key, extent, pieces, -0.22, 0.18) if pieces else 1.0
    values = jax.random.normal(stream_key, extent, jnp.float32) * scale * factor_of
    return jnp.minimum(jnp.maximum(values, -most), most).astype(kind)


def setup_inputs(seed: int = 0) -> dict:
    splits = jax.random.split(jax.random.key(seed), 8)
    forcing = bell_draw(splits[0], (MEMBERS, 2, NX, NY), 1.0, 6.0, ((0, 4), (2, 16), (3, 8)), jnp.float32)
    strength = jnp.clip(jnp.exp(math.log(2.0) - 1.89712 * jax.random.uniform(splits[1], (NX // 8, NY // 8), jnp.float32) ** levels(splits[1], (NX // 8, NY // 8), ((0, 16), (1, 8)), -0.2, 0.2)), 0.3, 2.0)
    mask = with_ends((jax.random.randint(splits[2], (NX, NY), 0, 10) < 9).astype(jnp.int32), jax.random.fold_in(splits[2], 1), 0, 1)
    send_cell = draw_send_cell(jax.random.fold_in(splits[7], 71), 0)
    send_code = with_ends(jax.random.randint(splits[4], (MEMBERS, N_GX, N_GY, ENTRIES), 0, 17), jax.random.fold_in(splits[4], 1), 0, 16).astype(jnp.int32)
    recv_buoy = with_ends(jax.random.randint(splits[5], (MEMBERS, N_GX, N_GY, ENTRIES), 0, BUOYS), jax.random.fold_in(splits[5], 1), 0, BUOYS - 1).astype(jnp.int32)
    observed = bell_draw(splits[6], (MEMBERS, N_GX, N_GY, 2, BUOYS), 1.0, 6.0, ((0, 4), (1, 16), (2, 8)), jnp.float32)
    return dict(forcing=forcing, strength=strength, mask=mask, send_cell=send_cell, send_code=send_code, recv_buoy=recv_buoy, observed=observed)


visc_scale = 0.2
relax = 0.6
step_size = 0.2
damping = 0.7


def padded(field):
    return jnp.pad(field, ((0, 0), (1, 1), (1, 1)))


def strains(velocity):
    pads = padded(velocity)
    along_x = pads[0]
    along_y = pads[1]
    strain_x = along_x[2:, 1:-1] - along_x[1:-1, 1:-1]
    strain_y = along_y[1:-1, 2:] - along_y[1:-1, 1:-1]
    shear_rate = (along_x[1:-1, 2:] - along_x[1:-1, 1:-1]) + (along_y[2:, 1:-1] - along_y[1:-1, 1:-1])
    return jnp.stack([strain_x, strain_y, shear_rate])


def forward_step(velocity, stress, visc, cover, tau):
    rates = strains(velocity)
    first = relax * stress[0] + visc * (rates[0] + rates[1])
    second = relax * stress[1] + 0.25 * visc * (rates[0] - rates[1])
    third = relax * stress[2] + 0.25 * visc * rates[2]
    pads = padded(jnp.stack([0.5 * (first + second), 0.5 * (first - second), third]))
    force_x = pads[0, 1:-1, 1:-1] - pads[0, :-2, 1:-1] + pads[2, 1:-1, 1:-1] - pads[2, 1:-1, :-2]
    force_y = pads[1, 1:-1, 1:-1] - pads[1, 1:-1, :-2] + pads[2, 1:-1, 1:-1] - pads[2, :-2, 1:-1]
    forces = jnp.stack([force_x, force_y])
    velocity = cover * (damping * velocity + step_size * (forces + tau))
    return velocity, jnp.stack([first, second, third]), rates


def adjoint_step(adj_vel, adj_stress, rates, visc, cover):
    pads = padded(cover * step_size * adj_vel)
    adj_nx = pads[0, 1:-1, 1:-1] - pads[0, 2:, 1:-1]
    adj_ny = pads[1, 1:-1, 1:-1] - pads[1, 1:-1, 2:]
    adj_third = pads[0, 1:-1, 1:-1] - pads[0, 1:-1, 2:] + pads[1, 1:-1, 1:-1] - pads[1, 2:, 1:-1]
    total_one = adj_stress[0] + 0.5 * (adj_nx + adj_ny)
    total_two = adj_stress[1] + 0.5 * (adj_nx - adj_ny)
    total_three = adj_stress[2] + adj_third
    dvisc = total_one * (rates[0] + rates[1]) + 0.25 * total_two * (rates[0] - rates[1]) + 0.25 * total_three * rates[2]
    hpad = padded(jnp.stack([visc * (total_one + 0.25 * total_two), visc * (total_one - 0.25 * total_two), 0.25 * visc * total_three]))
    adj_east = cover * damping * adj_vel[0] + (hpad[0, :-2, 1:-1] - hpad[0, 1:-1, 1:-1]) + (hpad[2, 1:-1, :-2] - hpad[2, 1:-1, 1:-1])
    adj_north = cover * damping * adj_vel[1] + (hpad[1, 1:-1, :-2] - hpad[1, 1:-1, 1:-1]) + (hpad[2, :-2, 1:-1] - hpad[2, 1:-1, 1:-1])
    return jnp.stack([adj_east, adj_north]), relax * jnp.stack([total_one, total_two, total_three]), dvisc


def buoy_sum(values, slots):
    return jax.ops.segment_sum(values.T, slots, num_segments=BUOYS).T


def cell_sum(values, cells):
    return jax.ops.segment_sum(values.T, cells, num_segments=CX * CY).T


def reference(forcing, strength, mask, send_cell, send_code, recv_buoy, observed):
    cover = mask.astype(jnp.float32)
    fine = jnp.repeat(jnp.repeat(strength, 8, axis=0), 8, axis=1)
    visc = visc_scale * fine * cover
    misfits = []
    gradient = jnp.zeros((NX // 8, NY // 8), jnp.float32)
    for member_index in range(MEMBERS):
        tau = forcing[member_index]
        velocity = jnp.zeros((2, NX, NY), jnp.float32)
        stress = jnp.zeros((3, NX, NY), jnp.float32)
        kept = []
        for step in range(SUBCYCLES):
            velocity, stress, rates = forward_step(velocity, stress, visc, cover, tau)
            kept.append(rates)
        tiles = velocity.reshape(2, N_GX, CX, N_GY, CY).transpose(1, 3, 0, 2, 4).reshape(N_GX, N_GY, 2, CX * CY)
        cells = send_cell[member_index]
        weights = send_code[member_index].astype(jnp.float32) / 16.0
        partial_value = jnp.take_along_axis(tiles, cells[:, :, None, :], axis=3) * weights[:, :, None, :]
        received = partial_value.reshape(N_GX, N_GY, 2, N_GY, CAP).transpose(0, 3, 2, 1, 4).reshape(N_GX, N_GY, 2, ENTRIES)
        slots = recv_buoy[member_index]
        summed = jax.vmap(jax.vmap(buoy_sum))(received, slots)
        misfit = summed - observed[member_index]
        misfits.append(misfit)
        back = jnp.take_along_axis(misfit, slots[:, :, None, :], axis=3)
        back = back.reshape(N_GX, N_GY, 2, N_GY, CAP).transpose(0, 3, 2, 1, 4).reshape(N_GX, N_GY, 2, ENTRIES)
        adj_tiles = jax.vmap(jax.vmap(cell_sum))(back * weights[:, :, None, :], cells)
        adj_vel = adj_tiles.reshape(N_GX, N_GY, 2, CX, CY).transpose(2, 0, 3, 1, 4).reshape(2, NX, NY)
        adj_stress = jnp.zeros((3, NX, NY), jnp.float32)
        fine_grad = jnp.zeros((NX, NY), jnp.float32)
        for step in range(SUBCYCLES - 1, -1, -1):
            adj_vel, adj_stress, dvisc = adjoint_step(adj_vel, adj_stress, kept[step], visc, cover)
            fine_grad = fine_grad + dvisc
        fine_grad = visc_scale * cover * fine_grad
        gradient = gradient + fine_grad.reshape(NX // 8, 8, NY // 8, 8).sum(axis=(1, 3))
    return jnp.stack(misfits), gradient
```

```python
import jax
import jax.numpy as jnp
from jax import lax
from jax.experimental import pallas as pl
from jax.experimental.pallas import tpu as pltpu
from jax.sharding import PartitionSpec as P

SUBCYCLES = 8
BUOYS = 256
HALO = 8
ROWS = 32
COLS = 128
WIN = ROWS + 2 * HALO
OWNERS = 8

visc_scale = 0.2
relax = 0.6
step_size = 0.2
damping = 0.7

f32 = jnp.float32
bf16 = jnp.bfloat16


def from_behind(x, axis, by):
    count = lax.axis_size(axis)
    pairs = [(i, i + by) for i in range(count) if 0 <= i + by < count]
    return lax.ppermute(x, axis, pairs)


def iota(shape, dim):
    return lax.broadcasted_iota(jnp.int32, shape, dim)


def split3(x):
    hi = x.astype(bf16).astype(f32)
    rest = x - hi
    mid = rest.astype(bf16).astype(f32)
    return hi, mid, rest - mid


def contract_last(a, b):
    return lax.dot_general(a, b, (((1,), (1,)), ((), ())), preferred_element_type=f32)


def tile_fields(forcing, strength, mask):
    cover = mask.astype(f32)
    spread = (iota((16, COLS), 1) // 8 == iota((16, COLS), 0)).astype(f32)
    wide = jnp.dot(strength, spread, precision=lax.Precision.HIGHEST, preferred_element_type=f32)
    fine = jnp.concatenate([jnp.broadcast_to(wide[i : i + 1], (8, COLS)) for i in range(ROWS // 8)], axis=0)
    return forcing[0], forcing[1], cover, visc_scale * fine * cover


def pack_kernel(forcing, strength, mask, recv, out):
    b = lax.axis_index("gy")
    fields = tile_fields(forcing[...], strength[...], mask[...])
    lane = iota((8, COLS), 1)
    left = jnp.zeros((8, COLS), f32)
    right = jnp.zeros((8, COLS), f32)
    for g in range(4):
        for f in range(4):
            at = 32 * g + 8 * f
            piece = fields[f][8 * g : 8 * g + 8]
            here = (lane >= at) & (lane < at + 8)
            left = jnp.where(here, pltpu.roll(piece, at, 1) if at else piece, left)
            right = jnp.where(here, pltpu.roll(piece, at + 8, 1), right)
    slots = recv[...].astype(f32)
    for d in range(OWNERS):
        out[d, 0:8, :] = jnp.where(d < b, left, right)
        for k, s in enumerate((max(d - 1, 0), d, min(d + 1, OWNERS - 1))):
            out[d, 8 + 4 * k : 12 + 4 * k, :] = slots[4 * s : 4 * s + 4]
        out[d, 20:24, :] = jnp.zeros((4, COLS), f32)


def widen_kernel(received, forcing, strength, mask, ext, first, last):
    b = lax.axis_index("gy")
    fields = tile_fields(forcing[...], strength[...], mask[...])
    lane = iota((8, COLS), 1)
    from_left = received[jnp.maximum(b - 1, 0), 0:8, :] * (b > 0).astype(f32)
    from_right = received[jnp.minimum(b + 1, OWNERS - 1), 0:8, :] * (b < OWNERS - 1).astype(f32)
    for f in range(4):
        ext[f, :, 0:COLS] = fields[f]
        for g in range(4):
            at = 32 * g + 8 * f
            low = pltpu.roll(from_right, (COLS - at) % COLS, 1) if at else from_right
            high = pltpu.roll(from_left, (120 - at) % COLS, 1)
            ext[f, 8 * g : 8 * g + 8, COLS:] = jnp.where(lane < 8, low, jnp.where(lane >= 120, high, 0.0))
    first[...] = ext[:, 0:8, :]
    last[...] = ext[:, ROWS - 8 : ROWS, :]


def next_row(x):
    return pltpu.roll(x, x.shape[0] - 1, 0)


def prev_row(x):
    return pltpu.roll(x, 1, 0)


def next_col(x):
    return pltpu.roll(x, x.shape[1] - 1, 1)


def prev_col(x):
    return pltpu.roll(x, 1, 1)


def forward_kernel(ext, above, below, cells, codes, received, observed, sums, rates, window, vel):
    b = lax.axis_index("gy")
    force_x, force_y, cover, visc = (
        jnp.concatenate([above[f], ext[f], below[f]], axis=0) for f in range(4)
    )
    window[0] = cover
    window[1] = visc
    tau_x = step_size * cover * force_x
    tau_y = step_size * cover * force_y
    big = (0.625 * step_size) * visc
    small = (0.375 * step_size) * visc
    quarter = (0.25 * step_size) * visc
    u, v = tau_x, tau_y
    nx = ny = s3 = None
    own = slice(HALO, HALO + ROWS)
    for step in range(SUBCYCLES - 1):
        ex = next_row(u) - u
        ey = next_col(v) - v
        sh = (next_col(u) - u) + (next_row(v) - v)
        rates[step, 0] = ex[own, :COLS]
        rates[step, 1] = ey[own, :COLS]
        rates[step, 2] = sh[own, :COLS]
        dx = big * ex + small * ey
        dy = small * ex + big * ey
        ds = quarter * sh
        nx = dx if nx is None else relax * nx + dx
        ny = dy if ny is None else relax * ny + dy
        s3 = ds if s3 is None else relax * s3 + ds
        fx = (nx - prev_row(nx)) + (s3 - prev_col(s3))
        fy = (ny - prev_col(ny)) + (s3 - prev_row(s3))
        u = damping * u + cover * fx + tau_x
        v = damping * v + cover * fy + tau_y
    vel[0] = u[own, :COLS]
    vel[1] = v[own, :COLS]

    cell = cells[...]
    row, col = cell // COLS, cell % COLS
    got_u = jnp.zeros((ROWS, COLS), f32)
    got_v = jnp.zeros((ROWS, COLS), f32)
    for r in range(ROWS):
        hit = row == r
        line_u = jnp.broadcast_to(vel[0, r : r + 1, :], (ROWS, COLS))
        line_v = jnp.broadcast_to(vel[1, r : r + 1, :], (ROWS, COLS))
        got_u = jnp.where(hit, jnp.take_along_axis(line_u, col, axis=1), got_u)
        got_v = jnp.where(hit, jnp.take_along_axis(line_v, col, axis=1), got_v)
    weight = codes[...].astype(f32) * (1.0 / 16.0)
    parts = split3(got_u * weight) + split3(got_v * weight)
    sub = iota((8, COLS), 0)
    slot_ids = iota((BUOYS, COLS), 0)
    blocks = []
    for d in range(OWNERS):
        lines = received[d, 12:16, :].astype(jnp.int32)
        base = 8 * (d // 2)
        left, right = [], []
        for i in range(4):
            keep = sub == 4 * (d % 2) + i
            left.append(
                jnp.concatenate([jnp.where(keep, p[base : base + 8], 0.0) for p in parts], axis=0).astype(bf16)
            )
            right.append((slot_ids == lines[i : i + 1, :]).astype(f32).astype(bf16))
        prod = contract_last(jnp.concatenate(left, axis=1), jnp.concatenate(right, axis=1))
        mine = (b == d).astype(f32)
        blocks.append(jnp.sum(prod[0:24], axis=0, keepdims=True) - mine * observed[0:1, :])
        blocks.append(jnp.sum(prod[24:48], axis=0, keepdims=True) - mine * observed[1:2, :])
    total = jnp.concatenate(blocks, axis=0)
    for d in range(OWNERS):
        sums[d] = total


def scatter_kernel(sums, tables, received, misfit, adj, first, last, total, lhs, rhs):
    b = lax.axis_index("gy")
    acc = sums[0]
    for j in range(1, OWNERS):
        acc = acc + sums[j]
    total[...] = acc
    mine = acc[0:2]
    for d in range(1, OWNERS):
        mine = jnp.where(b == d, acc[2 * d : 2 * d + 2], mine)
    misfit[...] = mine
    sub = iota((8, COLS), 0)
    lane = iota((ROWS, COLS), 1)
    row_ids = iota((ROWS, COLS), 0)
    col_ids = iota((COLS, COLS), 0)
    results = []
    for k, s in enumerate((jnp.maximum(b - 1, 0), b, jnp.minimum(b + 1, OWNERS - 1))):
        cell = tables[s, 0]
        weight = tables[s, 1].astype(f32) * (1.0 / 16.0)
        row, col = cell // COLS, cell % COLS
        values = [[], []]
        for q in range(4):
            slot = jnp.concatenate(
                [received[2 * q + o, 8 + 4 * k : 12 + 4 * k, :] for o in range(2)], axis=0
            ).astype(jnp.int32)
            near = slot % COLS
            for c in range(2):
                table = [
                    jnp.where(
                        sub < 4,
                        jnp.broadcast_to(total[4 * q + c : 4 * q + c + 1, h : h + COLS], (8, COLS)),
                        jnp.broadcast_to(total[4 * q + 2 + c : 4 * q + 3 + c, h : h + COLS], (8, COLS)),
                    )
                    for h in (0, COLS)
                ]
                values[c].append(
                    jnp.where(
                        slot < COLS,
                        jnp.take_along_axis(table[0], near, axis=1),
                        jnp.take_along_axis(table[1], near, axis=1),
                    )
                )
        parts = []
        for c in range(2):
            parts += split3(jnp.concatenate(values[c], axis=0) * weight)
        for i in range(ROWS):
            at = slice(COLS * i, COLS * i + COLS)
            hit = row_ids == row[i : i + 1, :]
            for p, part in enumerate(parts):
                lhs[ROWS * p : ROWS * p + ROWS, at] = jnp.where(hit, part[i : i + 1, :], 0.0).astype(bf16)
            rhs[:, at] = (col_ids == col[i : i + 1, :]).astype(f32).astype(bf16)
        prod = contract_last(lhs[...], rhs[...])
        results.append(
            [prod[96 * c : 96 * c + 32] + prod[96 * c + 32 : 96 * c + 64] + prod[96 * c + 64 : 96 * c + 96] for c in range(2)]
        )
    for c in range(2):
        adj[c, :, 0:COLS] = results[1][c]
        adj[c, :, COLS:] = jnp.where(lane < 8, results[2][c], jnp.where(lane >= 120, results[0][c], 0.0))
    first[...] = adj[:, 0:8, :]
    last[...] = adj[:, ROWS - 8 : ROWS, :]


def adjoint_kernel(adj, above, below, window, rates, out):
    cover = window[0]
    visc = window[1]
    scaled = step_size * cover
    third = 0.25 * visc
    w0, w1 = (scaled * jnp.concatenate([above[c], adj[c], below[c]], axis=0) for c in range(2))
    own = slice(HALO, HALO + ROWS)
    a = h = t = None
    grad = None
    for step in range(SUBCYCLES - 2, -1, -1):
        ax = w0 - next_row(w0)
        ay = w1 - next_col(w1)
        at = (w0 - next_col(w0)) + (w1 - next_row(w1))
        da = 0.625 * ax + 0.375 * ay
        dh = 0.375 * ax + 0.625 * ay
        a = da if a is None else relax * a + da
        h = dh if h is None else relax * h + dh
        t = at if t is None else relax * t + at
        term = (
            a[own, :COLS] * rates[step, 0]
            + h[own, :COLS] * rates[step, 1]
            + 0.25 * (t[own, :COLS] * rates[step, 2])
        )
        grad = term if grad is None else grad + term
        if step:
            ra, rh, rt = visc * a, visc * h, third * t
            w0 = damping * w0 + scaled * ((prev_row(ra) - ra) + (prev_col(rt) - rt))
            w1 = damping * w1 + scaled * ((prev_col(rh) - rh) + (prev_row(rt) - rt))
    grad = visc_scale * cover[own, :COLS] * grad
    rows = jnp.concatenate(
        [jnp.sum(grad[8 * i : 8 * i + 8], axis=0, keepdims=True) for i in range(ROWS // 8)], axis=0
    )
    gather = (iota((COLS, 16), 0) // 8 == iota((COLS, 16), 1)).astype(f32)
    out[...] = jnp.dot(rows, gather, precision=lax.Precision.HIGHEST, preferred_element_type=f32)


def call(kernel, outs, args, scratch=()):
    vmem = pl.BlockSpec(memory_space=pltpu.VMEM)
    return pl.pallas_call(
        kernel,
        out_shape=tuple(jax.ShapeDtypeStruct(s, f32) for s in outs),
        in_specs=[vmem] * len(args),
        out_specs=(vmem,) * len(outs),
        scratch_shapes=list(scratch),
        compiler_params=pltpu.CompilerParams(vmem_limit_bytes=24 * 1024 * 1024),
    )(*args)


def per_device(forcing, strength, mask, send_cell, send_code, recv_buoy, observed):
    forcing = forcing[0]
    cells = send_cell.reshape(ROWS, COLS)
    codes = send_code.reshape(ROWS, COLS)
    recv = recv_buoy.reshape(ROWS, COLS)
    observed = observed.reshape(2, BUOYS)
    tables = lax.all_gather(jnp.stack([cells, codes]), "gy")
    (packed,) = call(pack_kernel, [(OWNERS, 24, COLS)], (forcing, strength, mask, recv))
    received = lax.all_to_all(packed, "gy", 0, 0, tiled=True)
    ext, first, last = call(
        widen_kernel,
        [(4, ROWS, 2 * COLS), (4, 8, 2 * COLS), (4, 8, 2 * COLS)],
        (received, forcing, strength, mask),
    )
    above = from_behind(last, "gx", 1)
    below = from_behind(first, "gx", -1)
    sums, rates, window = call(
        forward_kernel,
        [(OWNERS, 2 * OWNERS, BUOYS), (SUBCYCLES - 1, 3, ROWS, COLS), (2, WIN, 2 * COLS)],
        (ext, above, below, cells, codes, received, observed),
        [pltpu.VMEM((2, ROWS, COLS), f32)],
    )
    sums = lax.all_to_all(sums, "gy", 0, 0, tiled=True)
    misfit, adj, first, last = call(
        scatter_kernel,
        [(2, BUOYS), (2, ROWS, 2 * COLS), (2, 8, 2 * COLS), (2, 8, 2 * COLS)],
        (sums, tables, received),
        [
            pltpu.VMEM((2 * OWNERS, BUOYS), f32),
            pltpu.VMEM((6 * ROWS, ROWS * COLS), bf16),
            pltpu.VMEM((COLS, ROWS * COLS), bf16),
        ],
    )
    above = from_behind(last, "gx", 1)
    below = from_behind(first, "gx", -1)
    (coarse,) = call(adjoint_kernel, [(ROWS // 8, COLS // 8)], (adj, above, below, window, rates))
    gradient = lax.psum(coarse, "member")
    return (misfit[None, None, None], gradient)


def solution(mesh):
    return jax.shard_map(
        per_device,
        mesh=mesh,
        in_specs=(
            P("member", None, "gx", "gy"),
            P("gx", "gy"),
            P("gx", "gy"),
            P("member", "gx", "gy", None),
            P("member", "gx", "gy", None),
            P("member", "gx", "gy", None),
            P("member", "gx", "gy", None, None),
        ),
        out_specs=(P("member", "gx", "gy", None, None), P("gx", "gy")),
        check_vma=False,
    )
```

```python
import jax
import jax.numpy as jnp
from jax import lax
from jax.experimental import pallas as pl
from jax.experimental.pallas import tpu as pltpu
from jax.sharding import PartitionSpec as P

SUBCYCLES = 8
BUOYS = 256
HALO = 8
ROWS = 32
COLS = 128
WIN = ROWS + 2 * HALO
OWNERS = 8
SPAN = 8

visc_scale = 0.2
relax = 0.6
step_size = 0.2
damping = 0.7

f32 = jnp.float32
bf16 = jnp.bfloat16


def from_behind(x, axis, by):
    count = lax.axis_size(axis)
    pairs = [(i, i + by) for i in range(count) if 0 <= i + by < count]
    return lax.ppermute(x, axis, pairs)


def iota(shape, dim):
    return lax.broadcasted_iota(jnp.int32, shape, dim)


def split3(x):
    hi = x.astype(bf16).astype(f32)
    rest = x - hi
    mid = rest.astype(bf16).astype(f32)
    return hi, mid, rest - mid


def contract_last(a, b):
    return lax.dot_general(a, b, (((1,), (1,)), ((), ())), preferred_element_type=f32)


def tile_fields(forcing, strength, mask):
    cover = mask.astype(f32)
    spread = (iota((16, COLS), 1) // 8 == iota((16, COLS), 0)).astype(f32)
    wide = jnp.dot(strength, spread, precision=lax.Precision.HIGHEST, preferred_element_type=f32)
    fine = jnp.concatenate([jnp.broadcast_to(wide[i : i + 1], (8, COLS)) for i in range(ROWS // 8)], axis=0)
    return forcing[0], forcing[1], cover, visc_scale * fine * cover


def pack_kernel(
    forcing_in, strength_in, mask_in, recv_in, cells_in, codes_in, observed_in,
    out, own, table, observed,
    forcing, strength, mask, recv, sems,
):
    b = lax.axis_index("gy")
    sources = (forcing_in, strength_in, mask_in, recv_in, cells_in, codes_in, observed_in)
    targets = (forcing, strength, mask, recv, table.at[0], table.at[1], observed)
    copies = [pltpu.make_async_copy(a, t, sems.at[i]) for i, (a, t) in enumerate(zip(sources, targets))]
    for copy in copies:
        copy.start()
    for copy in copies:
        copy.wait()
    fields = tile_fields(forcing[...], strength[...], mask[...])
    for f in range(4):
        own[f] = fields[f]
    lane = iota((8, COLS), 1)
    left = jnp.zeros((8, COLS), f32)
    right = jnp.zeros((8, COLS), f32)
    for g in range(4):
        for f in range(4):
            at = 32 * g + 8 * f
            piece = fields[f][8 * g : 8 * g + 8]
            here = (lane >= at) & (lane < at + 8)
            left = jnp.where(here, pltpu.roll(piece, at, 1) if at else piece, left)
            right = jnp.where(here, pltpu.roll(piece, at + 8, 1), right)
    slots = recv[...].astype(f32)
    for d in range(OWNERS):
        out[d, 0:8, :] = jnp.where(d < b, left, right)
        out[d, 8:12, :] = slots[4 * d : 4 * d + 4]


def widen_kernel(received, own, ext, first, last):
    b = lax.axis_index("gy")
    lane = iota((8, COLS), 1)
    from_left = received[jnp.maximum(b - 1, 0), 0:8, :] * (b > 0).astype(f32)
    from_right = received[jnp.minimum(b + 1, OWNERS - 1), 0:8, :] * (b < OWNERS - 1).astype(f32)
    for f in range(4):
        ext[f, :, 0:COLS] = own[f]
        for g in range(4):
            at = 32 * g + 8 * f
            low = pltpu.roll(from_right, (COLS - at) % COLS, 1) if at else from_right
            high = pltpu.roll(from_left, (120 - at) % COLS, 1)
            ext[f, 8 * g : 8 * g + 8, COLS:] = jnp.where(lane < 8, low, jnp.where(lane >= 120, high, 0.0))
    first[...] = ext[:, 0:8, :]
    last[...] = ext[:, ROWS - 8 : ROWS, :]


def next_row(x):
    return pltpu.roll(x, x.shape[0] - 1, 0)


def prev_row(x):
    return pltpu.roll(x, 1, 0)


def next_col(x):
    return pltpu.roll(x, x.shape[1] - 1, 1)


def prev_col(x):
    return pltpu.roll(x, 1, 1)


def own_kernel(received, table, table_out, slot_hot, col_hot):
    slot_ids = iota((BUOYS, COLS), 0)
    col_ids = iota((COLS, COLS), 0)
    slots = jnp.concatenate([received[d, 8:12, :] for d in range(OWNERS)], axis=0).astype(jnp.int32)
    cell = table[0]
    weight = table[1].astype(f32) * (1.0 / 16.0)
    col = cell % COLS
    table_out[0] = cell
    table_out[1] = table[1]
    table_out[2] = slots
    for i in range(ROWS):
        at = slice(COLS * i, COLS * i + COLS)
        slot_hot[:, at] = (slot_ids == slots[i : i + 1, :]).astype(f32).astype(bf16)
        col_hot[:, at] = jnp.where(col_ids == col[i : i + 1, :], weight[i : i + 1, :], 0.0).astype(bf16)


def forward_kernel(ext, above, below, hot, table, observed, sums, rates, window, vel):
    b = lax.axis_index("gy")
    force_x, force_y, cover, visc = (
        jnp.concatenate([above[f], ext[f], below[f]], axis=0) for f in range(4)
    )
    window[0] = cover
    window[1] = visc
    tau_x = step_size * cover * force_x
    tau_y = step_size * cover * force_y
    big = (0.625 * step_size) * visc
    small = (0.375 * step_size) * visc
    quarter = (0.25 * step_size) * visc
    u, v = tau_x, tau_y
    nx = ny = s3 = None
    own = slice(HALO, HALO + ROWS)
    for step in range(SUBCYCLES - 1):
        ex = next_row(u) - u
        ey = next_col(v) - v
        sh = (next_col(u) - u) + (next_row(v) - v)
        rates[step, 0] = ex[own, :COLS]
        rates[step, 1] = ey[own, :COLS]
        rates[step, 2] = sh[own, :COLS]
        dx = big * ex + small * ey
        dy = small * ex + big * ey
        ds = quarter * sh
        nx = dx if nx is None else relax * nx + dx
        ny = dy if ny is None else relax * ny + dy
        s3 = ds if s3 is None else relax * s3 + ds
        fx = (nx - prev_row(nx)) + (s3 - prev_col(s3))
        fy = (ny - prev_col(ny)) + (s3 - prev_row(s3))
        u = damping * u + cover * fx + tau_x
        v = damping * v + cover * fy + tau_y
    vel[0] = u[own, :COLS]
    vel[1] = v[own, :COLS]

    cell = table[0]
    row, col = cell // COLS, cell % COLS
    got_u = jnp.zeros((ROWS, COLS), f32)
    got_v = jnp.zeros((ROWS, COLS), f32)
    for r in range(ROWS):
        hit = row == r
        line_u = jnp.broadcast_to(vel[0, r : r + 1, :], (ROWS, COLS))
        line_v = jnp.broadcast_to(vel[1, r : r + 1, :], (ROWS, COLS))
        got_u = jnp.where(hit, jnp.take_along_axis(line_u, col, axis=1), got_u)
        got_v = jnp.where(hit, jnp.take_along_axis(line_v, col, axis=1), got_v)
    weight = table[1].astype(f32) * (1.0 / 16.0)
    parts = split3(got_u * weight) + split3(got_v * weight)
    sub = iota((8, COLS), 0)
    blocks = []
    for d in range(OWNERS):
        base = 8 * (d // 2)
        left = []
        for i in range(4):
            keep = sub == 4 * (d % 2) + i
            left.append(
                jnp.concatenate([jnp.where(keep, p[base : base + 8], 0.0) for p in parts], axis=0).astype(bf16)
            )
        prod = contract_last(jnp.concatenate(left, axis=1), hot[:, 4 * COLS * d : 4 * COLS * d + 4 * COLS])
        mine = (b == d).astype(f32)
        blocks.append(jnp.sum(prod[0:24], axis=0, keepdims=True) - mine * observed[0:1, :])
        blocks.append(jnp.sum(prod[24:48], axis=0, keepdims=True) - mine * observed[1:2, :])
    total = jnp.concatenate(blocks, axis=0)
    for d in range(OWNERS):
        sums[d] = total


def edge_kernel(left_table, right_table, left_hot, right_hot):
    edge_ids = iota((8 * SPAN, COLS), 0)
    for table, hot, first_col in ((left_table, left_hot, COLS - 8), (right_table, right_hot, 0)):
        cell = table[0]
        weight = table[1].astype(f32) * (1.0 / 16.0)
        row, col = cell // COLS, cell % COLS
        place = jnp.where((col >= first_col) & (col < first_col + 8), row % SPAN * 8 + col % 8, -1)
        for i in range(ROWS):
            at = slice(COLS * i, COLS * i + COLS)
            hot[:, at] = jnp.where(edge_ids == place[i : i + 1, :], weight[i : i + 1, :], 0.0).astype(bf16)


def scatter_kernel(
    sums, left_table, own_table, right_table, col_hot, left_hot, right_hot,
    misfit, adj, first, last,
    total, lhs, edge_lhs,
):
    b = lax.axis_index("gy")
    acc = sums[0]
    for j in range(1, OWNERS):
        acc = acc + sums[j]
    total[...] = acc
    mine = acc[0:2]
    for d in range(1, OWNERS):
        mine = jnp.where(b == d, acc[2 * d : 2 * d + 2], mine)
    misfit[...] = mine
    sub = iota((8, COLS), 0)
    lane = iota((8, COLS), 1)
    tables = [
        [
            [
                jnp.where(
                    sub < 4,
                    jnp.broadcast_to(total[4 * q + c : 4 * q + c + 1, h : h + COLS], (8, COLS)),
                    jnp.broadcast_to(total[4 * q + 2 + c : 4 * q + 3 + c, h : h + COLS], (8, COLS)),
                )
                for h in (0, COLS)
            ]
            for c in range(2)
        ]
        for q in range(4)
    ]
    row_ids = iota((ROWS, COLS), 0)
    halo = [None, None, None]
    for k in (0, 2, 1):
        row = (left_table, own_table, right_table)[k][0] // COLS
        values = [[], []]
        for q in range(4):
            slot = (left_table, own_table, right_table)[k][2, 8 * q : 8 * q + 8, :]
            near = slot % COLS
            for c in range(2):
                values[c].append(
                    jnp.where(
                        slot < COLS,
                        jnp.take_along_axis(tables[q][c][0], near, axis=1),
                        jnp.take_along_axis(tables[q][c][1], near, axis=1),
                    )
                )
        parts = []
        for c in range(2):
            parts += split3(jnp.concatenate(values[c], axis=0))
        if k == 1:
            for i in range(ROWS):
                at = slice(COLS * i, COLS * i + COLS)
                hit = row_ids == row[i : i + 1, :]
                for p, part in enumerate(parts):
                    lhs[ROWS * p : ROWS * p + ROWS, at] = jnp.where(hit, part[i : i + 1, :], 0.0).astype(bf16)
            prod = contract_last(lhs[...], col_hot[...])
            for c in range(2):
                at = 3 * ROWS * c
                adj[c, :, 0:COLS] = prod[at : at + 32] + prod[at + 32 : at + 64] + prod[at + 64 : at + 96]
        else:
            group = row // SPAN
            for i in range(ROWS):
                base = slice(8 * (i // 8), 8 * (i // 8) + 8)
                keep = [(sub == i % 8) & (group[base] == g) for g in range(ROWS // SPAN)]
                edge_lhs[:, COLS * i : COLS * i + COLS] = jnp.concatenate(
                    [jnp.where(m, p[base], 0.0) for m in keep for p in parts], axis=0
                ).astype(bf16)
            prod = contract_last(edge_lhs[...], (right_hot if k else left_hot)[...])
            halo[k] = [
                [jnp.sum(prod[at : at + 24], axis=0, keepdims=True) for at in (48 * g, 48 * g + 24)]
                for g in range(ROWS // SPAN)
            ]
    for c in range(2):
        for q in range(4):
            first_row = 8 * q % SPAN
            where = ((first_row % 16 + sub) * 8 + lane % 8) % COLS
            sides = []
            for k in (2, 0):
                line = halo[k][8 * q // SPAN][c]
                line = line[:, 8 * (first_row - first_row % 16) :][:, :COLS]
                if line.shape[1] < COLS:
                    line = jnp.concatenate([line, line], axis=1)
                sides.append(jnp.take_along_axis(jnp.broadcast_to(line, (8, COLS)), where, axis=1))
            adj[c, 8 * q : 8 * q + 8, COLS:] = jnp.where(lane < 8, sides[0], jnp.where(lane >= 120, sides[1], 0.0))
    first[...] = adj[:, 0:8, :]
    last[...] = adj[:, ROWS - 8 : ROWS, :]


def adjoint_kernel(adj, above, below, window, rates, out):
    cover = window[0]
    visc = window[1]
    scaled = step_size * cover
    third = 0.25 * visc
    w0, w1 = (scaled * jnp.concatenate([above[c], adj[c], below[c]], axis=0) for c in range(2))
    own = slice(HALO, HALO + ROWS)
    a = h = t = None
    grad = None
    for step in range(SUBCYCLES - 2, -1, -1):
        ax = w0 - next_row(w0)
        ay = w1 - next_col(w1)
        at = (w0 - next_col(w0)) + (w1 - next_row(w1))
        da = 0.625 * ax + 0.375 * ay
        dh = 0.375 * ax + 0.625 * ay
        a = da if a is None else relax * a + da
        h = dh if h is None else relax * h + dh
        t = at if t is None else relax * t + at
        term = (
            a[own, :COLS] * rates[step, 0]
            + h[own, :COLS] * rates[step, 1]
            + 0.25 * (t[own, :COLS] * rates[step, 2])
        )
        grad = term if grad is None else grad + term
        if step:
            ra, rh, rt = visc * a, visc * h, third * t
            w0 = damping * w0 + scaled * ((prev_row(ra) - ra) + (prev_col(rt) - rt))
            w1 = damping * w1 + scaled * ((prev_col(rh) - rh) + (prev_row(rt) - rt))
    grad = visc_scale * cover[own, :COLS] * grad
    rows = jnp.concatenate(
        [jnp.sum(grad[8 * i : 8 * i + 8], axis=0, keepdims=True) for i in range(ROWS // 8)], axis=0
    )
    gather = (iota((COLS, 16), 0) // 8 == iota((COLS, 16), 1)).astype(f32)
    out[...] = jnp.dot(rows, gather, precision=lax.Precision.HIGHEST, preferred_element_type=f32)


def call(kernel, outs, args, far=(), scratch=(), cost=0, limit=8):
    far = [pltpu.with_memory_space_constraint(x, pltpu.HBM) for x in far]
    near = pl.BlockSpec(memory_space=pltpu.VMEM)
    return pl.pallas_call(
        kernel,
        out_shape=tuple(outs),
        in_specs=[near] * len(args) + [pl.BlockSpec(memory_space=pltpu.HBM)] * len(far),
        out_specs=(near,) * len(outs),
        scratch_shapes=list(scratch),
        cost_estimate=pl.CostEstimate(flops=cost, bytes_accessed=0, transcendentals=0) if cost else None,
        compiler_params=pltpu.CompilerParams(vmem_limit_bytes=limit * 1024 * 1024),
    )(*args, *far)


def near(*shape, dtype=f32):
    return pltpu.VMEM(shape, dtype)


def per_device(forcing, strength, mask, send_cell, send_code, recv_buoy, observed):
    forcing = forcing[0]
    cells = send_cell.reshape(ROWS, COLS)
    codes = send_code.reshape(ROWS, COLS)
    recv = recv_buoy.reshape(ROWS, COLS)
    observed = observed.reshape(2, BUOYS)
    entries = ROWS * COLS
    packed, own, table, observed = call(
        pack_kernel,
        [near(OWNERS, 12, COLS), near(4, ROWS, COLS), near(2, ROWS, COLS, dtype=jnp.int32), near(2, BUOYS)],
        (),
        (forcing, strength, mask, recv, cells, codes, observed),
        [
            near(2, ROWS, COLS),
            near(ROWS // 8, COLS // 8),
            near(ROWS, COLS, dtype=jnp.int32),
            near(ROWS, COLS, dtype=jnp.int32),
            pltpu.SemaphoreType.DMA((7,)),
        ],
    )
    received = lax.all_to_all(packed, "gy", 0, 0, tiled=True)
    ext, first, last = call(
        widen_kernel,
        [near(4, ROWS, 2 * COLS), near(4, 8, 2 * COLS), near(4, 8, 2 * COLS)],
        (received, own),
    )
    above = from_behind(last, "gx", 1)
    below = from_behind(first, "gx", -1)
    table, slot_hot, col_hot = call(
        own_kernel,
        [
            near(3, ROWS, COLS, dtype=jnp.int32),
            near(BUOYS, entries, dtype=bf16),
            near(COLS, entries, dtype=bf16),
        ],
        (received, table),
        cost=10**9,
    )
    sums, rates, window = call(
        forward_kernel,
        [near(OWNERS, 2 * OWNERS, BUOYS), near(SUBCYCLES - 1, 3, ROWS, COLS), near(2, WIN, 2 * COLS)],
        (ext, above, below, slot_hot, table, observed),
        (),
        [near(2, ROWS, COLS)],
    )
    sums = lax.all_to_all(sums, "gy", 0, 0, tiled=True)
    left_table = from_behind(table, "gy", 1)
    right_table = from_behind(table, "gy", -1)
    left_hot, right_hot = call(
        edge_kernel,
        [near(8 * SPAN, entries, dtype=bf16), near(8 * SPAN, entries, dtype=bf16)],
        (left_table, right_table),
        cost=10**9,
    )
    misfit, adj, first, last = call(
        scatter_kernel,
        [
            jax.ShapeDtypeStruct((2, BUOYS), f32),
            near(2, ROWS, 2 * COLS),
            near(2, 8, 2 * COLS),
            near(2, 8, 2 * COLS),
        ],
        (sums, left_table, table, right_table, col_hot, left_hot, right_hot),
        (),
        [near(2 * OWNERS, BUOYS), near(6 * ROWS, entries, dtype=bf16), near(48 * ROWS // SPAN, entries, dtype=bf16)],
    )
    above = from_behind(last, "gx", 1)
    below = from_behind(first, "gx", -1)
    (coarse,) = call(adjoint_kernel, [near(ROWS // 8, COLS // 8)], (adj, above, below, window, rates))
    gradient = jnp.sum(lax.all_gather(coarse, "member"), axis=0)
    return (misfit[None, None, None], gradient)


def solution(mesh):
    return jax.shard_map(
        per_device,
        mesh=mesh,
        in_specs=(
            P("member", None, "gx", "gy"),
            P("gx", "gy"),
            P("gx", "gy"),
            P("member", "gx", "gy", None),
            P("member", "gx", "gy", None),
            P("member", "gx", "gy", None),
            P("member", "gx", "gy", None, None),
        ),
        out_specs=(P("member", "gx", "gy", None, None), P("gx", "gy")),
        check_vma=False,
    )
```

```python
import jax
import jax.numpy as jnp
from jax import lax
from jax.experimental import pallas as pl
from jax.experimental.pallas import tpu as pltpu
from jax.sharding import PartitionSpec as P

SUBCYCLES = 8
BUOYS = 256
HALO = 8
ROWS = 32
COLS = 128
WIN = ROWS + 2 * HALO
OWNERS = 8
SPAN = 8

visc_scale = 0.2
relax = 0.6
step_size = 0.2
damping = 0.7

f32 = jnp.float32
bf16 = jnp.bfloat16


def from_behind(x, axis, by):
    count = lax.axis_size(axis)
    pairs = [(i, i + by) for i in range(count) if 0 <= i + by < count]
    return lax.ppermute(x, axis, pairs)


def facing_rows(first, last):
    even = lax.axis_index("gx") % 2 == 0
    return jnp.where(even, last, first), jnp.where(even, first, last)


def above_below(pair, other, f):
    a = lax.axis_index("gx")
    near = pair[1 - a % 2, f]
    far = other[f]
    even = a % 2 == 0
    return jnp.where(even, far, near), jnp.where(even, near, far)


def exchange_rows(to_pair, to_other):
    count = lax.axis_size("gx")
    swaps = [(i, i + 1) for i in range(1, count - 1, 2)]
    other = lax.ppermute(to_other, "gx", swaps + [(j, i) for i, j in swaps])
    groups = [[i, i + 1] for i in range(0, count, 2)]
    pair = lax.all_gather(to_pair, "gx", axis_index_groups=groups)
    return pair, other


def iota(shape, dim):
    return lax.broadcasted_iota(jnp.int32, shape, dim)


def split3(x):
    hi = x.astype(bf16).astype(f32)
    rest = x - hi
    mid = rest.astype(bf16).astype(f32)
    return hi, mid, rest - mid


def contract_last(a, b):
    return lax.dot_general(a, b, (((1,), (1,)), ((), ())), preferred_element_type=f32)


def keep_parts(ref, parts):
    for p, part in enumerate(parts):
        ref[ROWS * p : ROWS * p + ROWS, :] = part
    ref[ROWS * len(parts) :, :] = jnp.zeros((ROWS * (8 - len(parts)), COLS), f32)


def parts_of_row(ref, i):
    return ref[pl.ds(i, 8, stride=ROWS), :]


def tile_fields(forcing, strength, mask):
    cover = mask.astype(f32)
    spread = (iota((16, COLS), 1) // 8 == iota((16, COLS), 0)).astype(f32)
    wide = jnp.dot(strength, spread, precision=lax.Precision.HIGHEST, preferred_element_type=f32)
    fine = jnp.concatenate([jnp.broadcast_to(wide[i : i + 1], (8, COLS)) for i in range(ROWS // 8)], axis=0)
    return forcing[0], forcing[1], cover, visc_scale * fine * cover


def pack_kernel(
    forcing_in, strength_in, mask_in, recv_in, cells_in, codes_in, observed_in,
    out, own, table, observed,
    forcing, strength, mask, recv, sems,
):
    b = lax.axis_index("gy")
    sources = (forcing_in, strength_in, mask_in, recv_in, cells_in, codes_in, observed_in)
    targets = (forcing, strength, mask, recv, table.at[0], table.at[1], observed)
    copies = [pltpu.make_async_copy(a, t, sems.at[i]) for i, (a, t) in enumerate(zip(sources, targets))]
    for copy in copies:
        copy.start()
    for copy in copies:
        copy.wait()
    fields = tile_fields(forcing[...], strength[...], mask[...])
    for f in range(4):
        own[f] = fields[f]
    lane = iota((8, COLS), 1)
    left = jnp.zeros((8, COLS), f32)
    right = jnp.zeros((8, COLS), f32)
    for g in range(4):
        for f in range(4):
            at = 32 * g + 8 * f
            piece = fields[f][8 * g : 8 * g + 8]
            here = (lane >= at) & (lane < at + 8)
            left = jnp.where(here, pltpu.roll(piece, at, 1) if at else piece, left)
            right = jnp.where(here, pltpu.roll(piece, at + 8, 1), right)
    slots = recv[...].astype(f32)
    for d in range(OWNERS):
        out[d, 0:8, :] = jnp.where(d < b, left, right)
        out[d, 8:12, :] = slots[4 * d : 4 * d + 4]


def widen_kernel(received, own, ext, to_pair, to_other):
    b = lax.axis_index("gy")
    lane = iota((8, COLS), 1)
    from_left = received[jnp.maximum(b - 1, 0), 0:8, :] * (b > 0).astype(f32)
    from_right = received[jnp.minimum(b + 1, OWNERS - 1), 0:8, :] * (b < OWNERS - 1).astype(f32)
    for f in range(4):
        ext[f, :, 0:COLS] = own[f]
        for g in range(4):
            at = 32 * g + 8 * f
            low = pltpu.roll(from_right, (COLS - at) % COLS, 1) if at else from_right
            high = pltpu.roll(from_left, (120 - at) % COLS, 1)
            ext[f, 8 * g : 8 * g + 8, COLS:] = jnp.where(lane < 8, low, jnp.where(lane >= 120, high, 0.0))
    to_pair[...], to_other[...] = facing_rows(ext[:, 0:8, :], ext[:, ROWS - 8 : ROWS, :])


def next_row(x):
    return pltpu.roll(x, x.shape[0] - 1, 0)


def prev_row(x):
    return pltpu.roll(x, 1, 0)


def next_col(x):
    return pltpu.roll(x, x.shape[1] - 1, 1)


def prev_col(x):
    return pltpu.roll(x, 1, 1)


def own_kernel(received, table, table_out, slot_hot, col_hot):
    slot_ids = iota((BUOYS, COLS), 0)
    col_ids = iota((COLS, COLS), 0)
    slots = jnp.concatenate([received[d, 8:12, :] for d in range(OWNERS)], axis=0).astype(jnp.int32)
    cell = table[0]
    weight = table[1].astype(f32) * (1.0 / 16.0)
    col = cell % COLS
    table_out[0] = cell
    table_out[1] = table[1]
    table_out[2] = slots
    for i in range(ROWS):
        at = slice(COLS * i, COLS * i + COLS)
        slot_hot[:, at] = (slot_ids == slots[i : i + 1, :]).astype(f32).astype(bf16)
        col_hot[:, at] = jnp.where(col_ids == col[i : i + 1, :], weight[i : i + 1, :], 0.0).astype(bf16)


def forward_kernel(ext, pair, other, hot, table, observed, sums, rates, window, vel, kept):
    b = lax.axis_index("gy")
    fields = []
    for f in range(4):
        above, below = above_below(pair, other, f)
        fields.append(jnp.concatenate([above, ext[f], below], axis=0))
    force_x, force_y, cover, visc = fields
    window[0] = cover
    window[1] = visc
    tau_x = step_size * cover * force_x
    tau_y = step_size * cover * force_y
    big = (0.625 * step_size) * visc
    small = (0.375 * step_size) * visc
    quarter = (0.25 * step_size) * visc
    u, v = tau_x, tau_y
    nx = ny = s3 = None
    own = slice(HALO, HALO + ROWS)
    for step in range(SUBCYCLES - 1):
        ex = next_row(u) - u
        ey = next_col(v) - v
        sh = (next_col(u) - u) + (next_row(v) - v)
        rates[step, 0] = ex[own, :COLS]
        rates[step, 1] = ey[own, :COLS]
        rates[step, 2] = sh[own, :COLS]
        dx = big * ex + small * ey
        dy = small * ex + big * ey
        ds = quarter * sh
        nx = dx if nx is None else relax * nx + dx
        ny = dy if ny is None else relax * ny + dy
        s3 = ds if s3 is None else relax * s3 + ds
        fx = (nx - prev_row(nx)) + (s3 - prev_col(s3))
        fy = (ny - prev_col(ny)) + (s3 - prev_row(s3))
        u = damping * u + cover * fx + tau_x
        v = damping * v + cover * fy + tau_y
    vel[0] = u[own, :COLS]
    vel[1] = v[own, :COLS]

    cell = table[0]
    row, col = cell // COLS, cell % COLS
    got_u = jnp.zeros((ROWS, COLS), f32)
    got_v = jnp.zeros((ROWS, COLS), f32)
    for r in range(ROWS):
        hit = row == r
        line_u = jnp.broadcast_to(vel[0, r : r + 1, :], (ROWS, COLS))
        line_v = jnp.broadcast_to(vel[1, r : r + 1, :], (ROWS, COLS))
        got_u = jnp.where(hit, jnp.take_along_axis(line_u, col, axis=1), got_u)
        got_v = jnp.where(hit, jnp.take_along_axis(line_v, col, axis=1), got_v)
    weight = table[1].astype(f32) * (1.0 / 16.0)
    keep_parts(kept, split3(got_u * weight) + split3(got_v * weight))
    blocks = []
    for d in range(OWNERS):
        left = jnp.concatenate([parts_of_row(kept, 4 * d + i) for i in range(4)], axis=1).astype(bf16)
        prod = contract_last(left, hot[:, 4 * COLS * d : 4 * COLS * d + 4 * COLS])
        mine = (b == d).astype(f32)
        blocks.append(jnp.sum(prod[0:3], axis=0, keepdims=True) - mine * observed[0:1, :])
        blocks.append(jnp.sum(prod[3:6], axis=0, keepdims=True) - mine * observed[1:2, :])
    total = jnp.concatenate(blocks, axis=0)
    for d in range(OWNERS):
        sums[d] = total


def edge_kernel(left_table, right_table, left_hot, right_hot):
    edge_ids = iota((8 * SPAN, COLS), 0)
    for table, hot, first_col in ((left_table, left_hot, COLS - 8), (right_table, right_hot, 0)):
        cell = table[0]
        weight = table[1].astype(f32) * (1.0 / 16.0)
        row, col = cell // COLS, cell % COLS
        place = jnp.where((col >= first_col) & (col < first_col + 8), row % SPAN * 8 + col % 8, -1)
        for i in range(ROWS):
            at = slice(COLS * i, COLS * i + COLS)
            hot[:, at] = jnp.where(edge_ids == place[i : i + 1, :], weight[i : i + 1, :], 0.0).astype(bf16)


def scatter_kernel(
    sums, left_table, own_table, right_table, col_hot, left_hot, right_hot,
    misfit, adj, to_pair, to_other,
    total, kept, lhs, edge_lhs,
):
    b = lax.axis_index("gy")
    acc = sums[0]
    for j in range(1, OWNERS):
        acc = acc + sums[j]
    total[...] = acc
    mine = acc[0:2]
    for d in range(1, OWNERS):
        mine = jnp.where(b == d, acc[2 * d : 2 * d + 2], mine)
    misfit[...] = mine
    sub = iota((8, COLS), 0)
    lane = iota((8, COLS), 1)
    tables = [
        [
            [
                jnp.where(
                    sub < 4,
                    jnp.broadcast_to(total[4 * q + c : 4 * q + c + 1, h : h + COLS], (8, COLS)),
                    jnp.broadcast_to(total[4 * q + 2 + c : 4 * q + 3 + c, h : h + COLS], (8, COLS)),
                )
                for h in (0, COLS)
            ]
            for c in range(2)
        ]
        for q in range(4)
    ]
    row_ids = iota((ROWS, COLS), 0)
    halo = [None, None, None]
    for k in (0, 2, 1):
        row = (left_table, own_table, right_table)[k][0] // COLS
        values = [[], []]
        for q in range(4):
            slot = (left_table, own_table, right_table)[k][2, 8 * q : 8 * q + 8, :]
            near = slot % COLS
            for c in range(2):
                values[c].append(
                    jnp.where(
                        slot < COLS,
                        jnp.take_along_axis(tables[q][c][0], near, axis=1),
                        jnp.take_along_axis(tables[q][c][1], near, axis=1),
                    )
                )
        parts = []
        for c in range(2):
            parts += split3(jnp.concatenate(values[c], axis=0))
        if k == 1:
            for i in range(ROWS):
                at = slice(COLS * i, COLS * i + COLS)
                hit = row_ids == row[i : i + 1, :]
                for p, part in enumerate(parts):
                    lhs[ROWS * p : ROWS * p + ROWS, at] = jnp.where(hit, part[i : i + 1, :], 0.0).astype(bf16)
            prod = contract_last(lhs[...], col_hot[...])
            for c in range(2):
                at = 3 * ROWS * c
                adj[c, :, 0:COLS] = prod[at : at + 32] + prod[at + 32 : at + 64] + prod[at + 64 : at + 96]
        else:
            keep_parts(kept.at[k // 2], parts)
            group = row // SPAN
            for i in range(ROWS):
                block = parts_of_row(kept.at[k // 2], i)
                edge_lhs[:, COLS * i : COLS * i + COLS] = jnp.concatenate(
                    [jnp.where(group[i : i + 1, :] == g, block, 0.0) for g in range(ROWS // SPAN)], axis=0
                ).astype(bf16)
            prod = contract_last(edge_lhs[...], (right_hot if k else left_hot)[...])
            halo[k] = [
                [jnp.sum(prod[at : at + 3], axis=0, keepdims=True) for at in (8 * g, 8 * g + 3)]
                for g in range(ROWS // SPAN)
            ]
    for c in range(2):
        for q in range(4):
            first_row = 8 * q % SPAN
            where = ((first_row % 16 + sub) * 8 + lane % 8) % COLS
            sides = []
            for k in (2, 0):
                line = halo[k][8 * q // SPAN][c]
                line = line[:, 8 * (first_row - first_row % 16) :][:, :COLS]
                if line.shape[1] < COLS:
                    line = jnp.concatenate([line, line], axis=1)
                sides.append(jnp.take_along_axis(jnp.broadcast_to(line, (8, COLS)), where, axis=1))
            adj[c, 8 * q : 8 * q + 8, COLS:] = jnp.where(lane < 8, sides[0], jnp.where(lane >= 120, sides[1], 0.0))
    to_pair[...], to_other[...] = facing_rows(adj[:, 0:8, :], adj[:, ROWS - 8 : ROWS, :])


def adjoint_kernel(adj, pair, other, window, rates, out):
    cover = window[0]
    visc = window[1]
    scaled = step_size * cover
    third = 0.25 * visc
    states = []
    for c in range(2):
        above, below = above_below(pair, other, c)
        states.append(scaled * jnp.concatenate([above, adj[c], below], axis=0))
    w0, w1 = states
    own = slice(HALO, HALO + ROWS)
    a = h = t = None
    grad = None
    for step in range(SUBCYCLES - 2, -1, -1):
        ax = w0 - next_row(w0)
        ay = w1 - next_col(w1)
        at = (w0 - next_col(w0)) + (w1 - next_row(w1))
        da = 0.625 * ax + 0.375 * ay
        dh = 0.375 * ax + 0.625 * ay
        a = da if a is None else relax * a + da
        h = dh if h is None else relax * h + dh
        t = at if t is None else relax * t + at
        term = (
            a[own, :COLS] * rates[step, 0]
            + h[own, :COLS] * rates[step, 1]
            + 0.25 * (t[own, :COLS] * rates[step, 2])
        )
        grad = term if grad is None else grad + term
        if step:
            ra, rh, rt = visc * a, visc * h, third * t
            w0 = damping * w0 + scaled * ((prev_row(ra) - ra) + (prev_col(rt) - rt))
            w1 = damping * w1 + scaled * ((prev_col(rh) - rh) + (prev_row(rt) - rt))
    grad = visc_scale * cover[own, :COLS] * grad
    rows = jnp.concatenate(
        [jnp.sum(grad[8 * i : 8 * i + 8], axis=0, keepdims=True) for i in range(ROWS // 8)], axis=0
    )
    gather = (iota((COLS, 16), 0) // 8 == iota((COLS, 16), 1)).astype(f32)
    out[...] = jnp.dot(rows, gather, precision=lax.Precision.HIGHEST, preferred_element_type=f32)


def call(kernel, outs, args, far=(), scratch=(), cost=0, limit=8):
    far = [pltpu.with_memory_space_constraint(x, pltpu.HBM) for x in far]
    near = pl.BlockSpec(memory_space=pltpu.VMEM)
    return pl.pallas_call(
        kernel,
        out_shape=tuple(outs),
        in_specs=[near] * len(args) + [pl.BlockSpec(memory_space=pltpu.HBM)] * len(far),
        out_specs=(near,) * len(outs),
        scratch_shapes=list(scratch),
        cost_estimate=pl.CostEstimate(flops=cost, bytes_accessed=0, transcendentals=0) if cost else None,
        compiler_params=pltpu.CompilerParams(vmem_limit_bytes=limit * 1024 * 1024),
    )(*args, *far)


def near(*shape, dtype=f32):
    return pltpu.VMEM(shape, dtype)


def per_device(forcing, strength, mask, send_cell, send_code, recv_buoy, observed):
    forcing = forcing[0]
    cells = send_cell.reshape(ROWS, COLS)
    codes = send_code.reshape(ROWS, COLS)
    recv = recv_buoy.reshape(ROWS, COLS)
    observed = observed.reshape(2, BUOYS)
    entries = ROWS * COLS
    packed, own, table, observed = call(
        pack_kernel,
        [near(OWNERS, 12, COLS), near(4, ROWS, COLS), near(2, ROWS, COLS, dtype=jnp.int32), near(2, BUOYS)],
        (),
        (forcing, strength, mask, recv, cells, codes, observed),
        [
            near(2, ROWS, COLS),
            near(ROWS // 8, COLS // 8),
            near(ROWS, COLS, dtype=jnp.int32),
            near(ROWS, COLS, dtype=jnp.int32),
            pltpu.SemaphoreType.DMA((7,)),
        ],
    )
    received = lax.all_to_all(packed, "gy", 0, 0, tiled=True)
    ext, to_pair, to_other = call(
        widen_kernel,
        [near(4, ROWS, 2 * COLS), near(4, 8, 2 * COLS), near(4, 8, 2 * COLS)],
        (received, own),
    )
    pair, other = exchange_rows(to_pair, to_other)
    table, slot_hot, col_hot = call(
        own_kernel,
        [
            near(3, ROWS, COLS, dtype=jnp.int32),
            near(BUOYS, entries, dtype=bf16),
            near(COLS, entries, dtype=bf16),
        ],
        (received, table),
        cost=10**9,
    )
    sums, rates, window = call(
        forward_kernel,
        [near(OWNERS, 2 * OWNERS, BUOYS), near(SUBCYCLES - 1, 3, ROWS, COLS), near(2, WIN, 2 * COLS)],
        (ext, pair, other, slot_hot, table, observed),
        (),
        [near(2, ROWS, COLS), near(8 * ROWS, COLS)],
    )
    sums = lax.all_to_all(sums, "gy", 0, 0, tiled=True)
    left_table = from_behind(table, "gy", 1)
    right_table = from_behind(table, "gy", -1)
    left_hot, right_hot = call(
        edge_kernel,
        [near(8 * SPAN, entries, dtype=bf16), near(8 * SPAN, entries, dtype=bf16)],
        (left_table, right_table),
        cost=10**9,
    )
    misfit, adj, to_pair, to_other = call(
        scatter_kernel,
        [
            jax.ShapeDtypeStruct((2, BUOYS), f32),
            near(2, ROWS, 2 * COLS),
            near(2, 8, 2 * COLS),
            near(2, 8, 2 * COLS),
        ],
        (sums, left_table, table, right_table, col_hot, left_hot, right_hot),
        (),
        [
            near(2 * OWNERS, BUOYS),
            near(2, 8 * ROWS, COLS),
            near(6 * ROWS, entries, dtype=bf16),
            near(8 * ROWS // SPAN, entries, dtype=bf16),
        ],
    )
    pair, other = exchange_rows(to_pair, to_other)
    (coarse,) = call(adjoint_kernel, [near(ROWS // 8, COLS // 8)], (adj, pair, other, window, rates))
    gradient = jnp.sum(lax.all_gather(coarse, "member"), axis=0)
    return (misfit[None, None, None], gradient)


def solution(mesh):
    return jax.shard_map(
        per_device,
        mesh=mesh,
        in_specs=(
            P("member", None, "gx", "gy"),
            P("gx", "gy"),
            P("gx", "gy"),
            P("member", "gx", "gy", None),
            P("member", "gx", "gy", None),
            P("member", "gx", "gy", None),
            P("member", "gx", "gy", None, None),
        ),
        out_specs=(P("member", "gx", "gy", None, None), P("gx", "gy")),
        check_vma=False,
    )
```

```python
import jax
import jax.numpy as jnp
from jax import lax
from jax.experimental import pallas as pl
from jax.experimental.pallas import tpu as pltpu
from jax.sharding import PartitionSpec as P

SUBCYCLES = 8
BUOYS = 256
HALO = 8
ROWS = 32
COLS = 128
WIN = ROWS + 2 * HALO
OWNERS = 8
SPAN = 8

visc_scale = 0.2
relax = 0.6
step_size = 0.2
damping = 0.7

f32 = jnp.float32
bf16 = jnp.bfloat16


def from_behind(x, axis, by):
    count = lax.axis_size(axis)
    pairs = [(i, i + by) for i in range(count) if 0 <= i + by < count]
    return lax.ppermute(x, axis, pairs)


def facing_rows(first, last):
    even = lax.axis_index("gx") % 2 == 0
    return jnp.where(even, last, first), jnp.where(even, first, last)


def above_below(pair, other, f):
    a = lax.axis_index("gx")
    near = pair[1 - a % 2, f]
    far = other[f]
    even = a % 2 == 0
    return jnp.where(even, far, near), jnp.where(even, near, far)


def exchange_rows(to_pair, to_other):
    count = lax.axis_size("gx")
    swaps = [(i, i + 1) for i in range(1, count - 1, 2)]
    other = lax.ppermute(to_other, "gx", swaps + [(j, i) for i, j in swaps])
    groups = [[i, i + 1] for i in range(0, count, 2)]
    pair = lax.all_gather(to_pair, "gx", axis_index_groups=groups)
    return pair, other


def iota(shape, dim):
    return lax.broadcasted_iota(jnp.int32, shape, dim)


def split3(x):
    hi = x.astype(bf16).astype(f32)
    rest = x - hi
    mid = rest.astype(bf16).astype(f32)
    return hi, mid, rest - mid


def contract_last(a, b):
    return lax.dot_general(a, b, (((1,), (1,)), ((), ())), preferred_element_type=f32)


def keep_parts(ref, parts):
    for p, part in enumerate(parts):
        ref[ROWS * p : ROWS * p + ROWS, :] = part
    ref[ROWS * len(parts) :, :] = jnp.zeros((ROWS * (8 - len(parts)), COLS), f32)


def parts_of_row(ref, i):
    return ref[pl.ds(i, 8, stride=ROWS), :]


def tile_fields(forcing, strength, mask):
    cover = mask.astype(f32)
    spread = (iota((16, COLS), 1) // 8 == iota((16, COLS), 0)).astype(f32)
    wide = jnp.dot(strength, spread, precision=lax.Precision.HIGHEST, preferred_element_type=f32)
    fine = jnp.concatenate([jnp.broadcast_to(wide[i : i + 1], (8, COLS)) for i in range(ROWS // 8)], axis=0)
    return forcing[0], forcing[1], cover, visc_scale * fine * cover


def pack_kernel(
    forcing_in, strength_in, mask_in, recv_in, cells_in, codes_in, observed_in,
    out, own, table, observed,
    forcing, strength, mask, recv, sems,
):
    b = lax.axis_index("gy")
    sources = (forcing_in, strength_in, mask_in, recv_in, cells_in, codes_in, observed_in)
    targets = (forcing, strength, mask, recv, table.at[0], table.at[1], observed)
    copies = [pltpu.make_async_copy(a, t, sems.at[i]) for i, (a, t) in enumerate(zip(sources, targets))]
    for copy in copies:
        copy.start()
    for copy in copies:
        copy.wait()
    fields = tile_fields(forcing[...], strength[...], mask[...])
    for f in range(4):
        own[f] = fields[f]
    lane = iota((8, COLS), 1)
    left = jnp.zeros((8, COLS), f32)
    right = jnp.zeros((8, COLS), f32)
    for g in range(4):
        for f in range(4):
            at = 32 * g + 8 * f
            piece = fields[f][8 * g : 8 * g + 8]
            here = (lane >= at) & (lane < at + 8)
            left = jnp.where(here, pltpu.roll(piece, at, 1) if at else piece, left)
            right = jnp.where(here, pltpu.roll(piece, at + 8, 1), right)
    slots = recv[...].astype(f32)
    for d in range(OWNERS):
        out[d, 0:8, :] = jnp.where(d < b, left, right)
        out[d, 8:12, :] = slots[4 * d : 4 * d + 4]


def widen_kernel(received, own, ext, to_pair, to_other):
    b = lax.axis_index("gy")
    lane = iota((8, COLS), 1)
    from_left = received[jnp.maximum(b - 1, 0), 0:8, :] * (b > 0).astype(f32)
    from_right = received[jnp.minimum(b + 1, OWNERS - 1), 0:8, :] * (b < OWNERS - 1).astype(f32)
    for f in range(4):
        ext[f, :, 0:COLS] = own[f]
        for g in range(4):
            at = 32 * g + 8 * f
            low = pltpu.roll(from_right, (COLS - at) % COLS, 1) if at else from_right
            high = pltpu.roll(from_left, (120 - at) % COLS, 1)
            ext[f, 8 * g : 8 * g + 8, COLS:] = jnp.where(lane < 8, low, jnp.where(lane >= 120, high, 0.0))
    to_pair[...], to_other[...] = facing_rows(ext[:, 0:8, :], ext[:, ROWS - 8 : ROWS, :])


def next_row(x):
    return pltpu.roll(x, x.shape[0] - 1, 0)


def prev_row(x):
    return pltpu.roll(x, 1, 0)


def next_col(x):
    return pltpu.roll(x, x.shape[1] - 1, 1)


def prev_col(x):
    return pltpu.roll(x, 1, 1)


def forward_kernel(ext, pair, other, received, table, observed, sums, rates, window, table_out, vel, kept, hot, total, sems):
    b = lax.axis_index("gy")
    slot_ids = iota((BUOYS, COLS), 0)
    slots = jnp.concatenate([received[d, 8:12, :] for d in range(OWNERS)], axis=0).astype(jnp.int32)
    table_out[0] = table[0]
    table_out[1] = table[1]
    table_out[2] = slots
    for i in range(ROWS):
        at = slice(COLS * i, COLS * i + COLS)
        hot[:, at] = (slot_ids == slots[i : i + 1, :]).astype(f32).astype(bf16)
    fields = []
    for f in range(4):
        above, below = above_below(pair, other, f)
        fields.append(jnp.concatenate([above, ext[f], below], axis=0))
    force_x, force_y, cover, visc = fields
    window[0] = cover
    window[1] = visc
    tau_x = step_size * cover * force_x
    tau_y = step_size * cover * force_y
    big = (0.625 * step_size) * visc
    small = (0.375 * step_size) * visc
    quarter = (0.25 * step_size) * visc
    u, v = tau_x, tau_y
    nx = ny = s3 = None
    own = slice(HALO, HALO + ROWS)
    for step in range(SUBCYCLES - 1):
        ex = next_row(u) - u
        ey = next_col(v) - v
        sh = (next_col(u) - u) + (next_row(v) - v)
        rates[step, 0] = ex[own, :COLS]
        rates[step, 1] = ey[own, :COLS]
        rates[step, 2] = sh[own, :COLS]
        dx = big * ex + small * ey
        dy = small * ex + big * ey
        ds = quarter * sh
        nx = dx if nx is None else relax * nx + dx
        ny = dy if ny is None else relax * ny + dy
        s3 = ds if s3 is None else relax * s3 + ds
        fx = (nx - prev_row(nx)) + (s3 - prev_col(s3))
        fy = (ny - prev_col(ny)) + (s3 - prev_row(s3))
        u = damping * u + cover * fx + tau_x
        v = damping * v + cover * fy + tau_y
    vel[0] = u[own, :COLS]
    vel[1] = v[own, :COLS]

    cell = table[0]
    row, col = cell // COLS, cell % COLS
    got_u = jnp.zeros((ROWS, COLS), f32)
    got_v = jnp.zeros((ROWS, COLS), f32)
    for r in range(ROWS):
        hit = row == r
        line_u = jnp.broadcast_to(vel[0, r : r + 1, :], (ROWS, COLS))
        line_v = jnp.broadcast_to(vel[1, r : r + 1, :], (ROWS, COLS))
        got_u = jnp.where(hit, jnp.take_along_axis(line_u, col, axis=1), got_u)
        got_v = jnp.where(hit, jnp.take_along_axis(line_v, col, axis=1), got_v)
    weight = table[1].astype(f32) * (1.0 / 16.0)
    keep_parts(kept, split3(got_u * weight) + split3(got_v * weight))
    blocks = []
    for d in range(OWNERS):
        left = jnp.concatenate([parts_of_row(kept, 4 * d + i) for i in range(4)], axis=1).astype(bf16)
        prod = contract_last(left, hot[:, 4 * COLS * d : 4 * COLS * d + 4 * COLS])
        mine = (b == d).astype(f32)
        blocks.append(jnp.sum(prod[0:3], axis=0, keepdims=True) - mine * observed[0:1, :])
        blocks.append(jnp.sum(prod[3:6], axis=0, keepdims=True) - mine * observed[1:2, :])
    total[...] = jnp.concatenate(blocks, axis=0)
    copies = [pltpu.make_async_copy(total, sums.at[d], sems.at[d]) for d in range(OWNERS)]
    for copy in copies:
        copy.start()
    for copy in copies:
        copy.wait()


def edge_kernel(own_table, left_table, right_table, col_hot, left_hot, right_hot):
    edge_ids = iota((8 * SPAN, COLS), 0)
    col_ids = iota((COLS, COLS), 0)
    for table, hot, first_col in ((own_table, col_hot, None), (left_table, left_hot, COLS - 8), (right_table, right_hot, 0)):
        cell = table[0]
        weight = table[1].astype(f32) * (1.0 / 16.0)
        row, col = cell // COLS, cell % COLS
        ids, place = col_ids, col
        if first_col is not None:
            ids = edge_ids
            place = jnp.where((col >= first_col) & (col < first_col + 8), row % SPAN * 8 + col % 8, -1)
        for i in range(ROWS):
            at = slice(COLS * i, COLS * i + COLS)
            hot[:, at] = jnp.where(ids == place[i : i + 1, :], weight[i : i + 1, :], 0.0).astype(bf16)


def scatter_kernel(
    sums, left_table, own_table, right_table, col_hot, left_hot, right_hot,
    misfit, adj, to_pair, to_other,
    total, kept, lhs, edge_lhs,
):
    b = lax.axis_index("gy")
    acc = sums[0]
    for j in range(1, OWNERS):
        acc = acc + sums[j]
    total[...] = acc
    mine = acc[0:2]
    for d in range(1, OWNERS):
        mine = jnp.where(b == d, acc[2 * d : 2 * d + 2], mine)
    misfit[...] = mine
    sub = iota((8, COLS), 0)
    lane = iota((8, COLS), 1)
    tables = [
        [
            [
                jnp.where(
                    sub < 4,
                    jnp.broadcast_to(total[4 * q + c : 4 * q + c + 1, h : h + COLS], (8, COLS)),
                    jnp.broadcast_to(total[4 * q + 2 + c : 4 * q + 3 + c, h : h + COLS], (8, COLS)),
                )
                for h in (0, COLS)
            ]
            for c in range(2)
        ]
        for q in range(4)
    ]
    row_ids = iota((ROWS, COLS), 0)
    halo = [None, None, None]
    for k in (0, 2, 1):
        row = (left_table, own_table, right_table)[k][0] // COLS
        values = [[], []]
        for q in range(4):
            slot = (left_table, own_table, right_table)[k][2, 8 * q : 8 * q + 8, :]
            near = slot % COLS
            for c in range(2):
                values[c].append(
                    jnp.where(
                        slot < COLS,
                        jnp.take_along_axis(tables[q][c][0], near, axis=1),
                        jnp.take_along_axis(tables[q][c][1], near, axis=1),
                    )
                )
        parts = []
        for c in range(2):
            parts += split3(jnp.concatenate(values[c], axis=0))
        if k == 1:
            for i in range(ROWS):
                at = slice(COLS * i, COLS * i + COLS)
                hit = row_ids == row[i : i + 1, :]
                for p, part in enumerate(parts):
                    lhs[ROWS * p : ROWS * p + ROWS, at] = jnp.where(hit, part[i : i + 1, :], 0.0).astype(bf16)
            prod = contract_last(lhs[...], col_hot[...])
            for c in range(2):
                at = 3 * ROWS * c
                adj[c, :, 0:COLS] = prod[at : at + 32] + prod[at + 32 : at + 64] + prod[at + 64 : at + 96]
        else:
            keep_parts(kept.at[k // 2], parts)
            group = row // SPAN
            for i in range(ROWS):
                block = parts_of_row(kept.at[k // 2], i)
                edge_lhs[:, COLS * i : COLS * i + COLS] = jnp.concatenate(
                    [jnp.where(group[i : i + 1, :] == g, block, 0.0) for g in range(ROWS // SPAN)], axis=0
                ).astype(bf16)
            prod = contract_last(edge_lhs[...], (right_hot if k else left_hot)[...])
            halo[k] = [
                [jnp.sum(prod[at : at + 3], axis=0, keepdims=True) for at in (8 * g, 8 * g + 3)]
                for g in range(ROWS // SPAN)
            ]
    for c in range(2):
        for q in range(4):
            first_row = 8 * q % SPAN
            where = ((first_row % 16 + sub) * 8 + lane % 8) % COLS
            sides = []
            for k in (2, 0):
                line = halo[k][8 * q // SPAN][c]
                line = line[:, 8 * (first_row - first_row % 16) :][:, :COLS]
                if line.shape[1] < COLS:
                    line = jnp.concatenate([line, line], axis=1)
                sides.append(jnp.take_along_axis(jnp.broadcast_to(line, (8, COLS)), where, axis=1))
            adj[c, 8 * q : 8 * q + 8, COLS:] = jnp.where(lane < 8, sides[0], jnp.where(lane >= 120, sides[1], 0.0))
    to_pair[...], to_other[...] = facing_rows(adj[:, 0:8, :], adj[:, ROWS - 8 : ROWS, :])


def adjoint_kernel(adj, pair, other, window, rates, misfit, out, misfit_out, sem):
    copy = pltpu.make_async_copy(misfit, misfit_out, sem.at[0])
    copy.start()
    cover = window[0]
    visc = window[1]
    scaled = step_size * cover
    third = 0.25 * visc
    states = []
    for c in range(2):
        above, below = above_below(pair, other, c)
        states.append(scaled * jnp.concatenate([above, adj[c], below], axis=0))
    w0, w1 = states
    own = slice(HALO, HALO + ROWS)
    a = h = t = None
    grad = None
    for step in range(SUBCYCLES - 2, -1, -1):
        ax = w0 - next_row(w0)
        ay = w1 - next_col(w1)
        at = (w0 - next_col(w0)) + (w1 - next_row(w1))
        da = 0.625 * ax + 0.375 * ay
        dh = 0.375 * ax + 0.625 * ay
        a = da if a is None else relax * a + da
        h = dh if h is None else relax * h + dh
        t = at if t is None else relax * t + at
        term = (
            a[own, :COLS] * rates[step, 0]
            + h[own, :COLS] * rates[step, 1]
            + 0.25 * (t[own, :COLS] * rates[step, 2])
        )
        grad = term if grad is None else grad + term
        if step:
            ra, rh, rt = visc * a, visc * h, third * t
            w0 = damping * w0 + scaled * ((prev_row(ra) - ra) + (prev_col(rt) - rt))
            w1 = damping * w1 + scaled * ((prev_col(rh) - rh) + (prev_row(rt) - rt))
    grad = visc_scale * cover[own, :COLS] * grad
    rows = jnp.concatenate(
        [jnp.sum(grad[8 * i : 8 * i + 8], axis=0, keepdims=True) for i in range(ROWS // 8)], axis=0
    )
    gather = (iota((COLS, 16), 0) // 8 == iota((COLS, 16), 1)).astype(f32)
    out[...] = jnp.dot(rows, gather, precision=lax.Precision.HIGHEST, preferred_element_type=f32)
    copy.wait()


def call(kernel, outs, args, far=(), scratch=(), cost=0, limit=8):
    far = [pltpu.with_memory_space_constraint(x, pltpu.HBM) for x in far]
    near = pl.BlockSpec(memory_space=pltpu.VMEM)
    return pl.pallas_call(
        kernel,
        out_shape=tuple(outs),
        in_specs=[near] * len(args) + [pl.BlockSpec(memory_space=pltpu.HBM)] * len(far),
        out_specs=tuple(pl.BlockSpec(memory_space=o.memory_space) for o in outs),
        scratch_shapes=list(scratch),
        cost_estimate=pl.CostEstimate(flops=cost, bytes_accessed=0, transcendentals=0) if cost else None,
        compiler_params=pltpu.CompilerParams(vmem_limit_bytes=limit * 1024 * 1024),
    )(*args, *far)


def near(*shape, dtype=f32):
    return pltpu.VMEM(shape, dtype)


def per_device(forcing, strength, mask, send_cell, send_code, recv_buoy, observed):
    forcing = forcing[0]
    cells = send_cell.reshape(ROWS, COLS)
    codes = send_code.reshape(ROWS, COLS)
    recv = recv_buoy.reshape(ROWS, COLS)
    observed = observed.reshape(2, BUOYS)
    entries = ROWS * COLS
    packed, own, table, observed = call(
        pack_kernel,
        [near(OWNERS, 12, COLS), near(4, ROWS, COLS), near(2, ROWS, COLS, dtype=jnp.int32), near(2, BUOYS)],
        (),
        (forcing, strength, mask, recv, cells, codes, observed),
        [
            near(2, ROWS, COLS),
            near(ROWS // 8, COLS // 8),
            near(ROWS, COLS, dtype=jnp.int32),
            near(ROWS, COLS, dtype=jnp.int32),
            pltpu.SemaphoreType.DMA((7,)),
        ],
    )
    received = lax.all_to_all(packed, "gy", 0, 0, tiled=True)
    ext, to_pair, to_other = call(
        widen_kernel,
        [near(4, ROWS, 2 * COLS), near(4, 8, 2 * COLS), near(4, 8, 2 * COLS)],
        (received, own),
    )
    pair, other = exchange_rows(to_pair, to_other)
    sums, rates, window, table = call(
        forward_kernel,
        [
            pltpu.HBM((OWNERS, 2 * OWNERS, BUOYS), f32),
            near(SUBCYCLES - 1, 3, ROWS, COLS),
            near(2, WIN, 2 * COLS),
            near(3, ROWS, COLS, dtype=jnp.int32),
        ],
        (ext, pair, other, received, table, observed),
        (),
        [
            near(2, ROWS, COLS),
            near(8 * ROWS, COLS),
            near(BUOYS, entries, dtype=bf16),
            near(2 * OWNERS, BUOYS),
            pltpu.SemaphoreType.DMA((OWNERS,)),
        ],
    )
    sums = lax.all_to_all(sums, "gy", 0, 0, tiled=True)
    left_table = from_behind(table, "gy", 1)
    right_table = from_behind(table, "gy", -1)
    col_hot, left_hot, right_hot = call(
        edge_kernel,
        [near(COLS, entries, dtype=bf16), near(8 * SPAN, entries, dtype=bf16), near(8 * SPAN, entries, dtype=bf16)],
        (table, left_table, right_table),
        cost=10**9,
    )
    misfit, adj, to_pair, to_other = call(
        scatter_kernel,
        [
            near(2, BUOYS),
            near(2, ROWS, 2 * COLS),
            near(2, 8, 2 * COLS),
            near(2, 8, 2 * COLS),
        ],
        (sums, left_table, table, right_table, col_hot, left_hot, right_hot),
        (),
        [
            near(2 * OWNERS, BUOYS),
            near(2, 8 * ROWS, COLS),
            near(6 * ROWS, entries, dtype=bf16),
            near(8 * ROWS // SPAN, entries, dtype=bf16),
        ],
    )
    pair, other = exchange_rows(to_pair, to_other)
    coarse, misfit = call(
        adjoint_kernel,
        [near(ROWS // 8, COLS // 8), pltpu.HBM((2, BUOYS), f32)],
        (adj, pair, other, window, rates, misfit),
        (),
        [pltpu.SemaphoreType.DMA((1,))],
    )
    gradient = jnp.sum(lax.all_gather(coarse, "member"), axis=0)
    return (misfit[None, None, None], gradient)


def solution(mesh):
    return jax.shard_map(
        per_device,
        mesh=mesh,
        in_specs=(
            P("member", None, "gx", "gy"),
            P("gx", "gy"),
            P("gx", "gy"),
            P("member", "gx", "gy", None),
            P("member", "gx", "gy", None),
            P("member", "gx", "gy", None),
            P("member", "gx", "gy", None, None),
        ),
        out_specs=(P("member", "gx", "gy", None, None), P("gx", "gy")),
        check_vma=False,
    )
```

```python
import jax
import jax.numpy as jnp
from jax import lax
from jax.experimental import pallas as pl
from jax.experimental.pallas import tpu as pltpu
from jax.sharding import PartitionSpec as P

SUBCYCLES = 8
BUOYS = 256
HALO = 8
ROWS = 32
COLS = 128
WIN = ROWS + 2 * HALO
OWNERS = 8
SPAN = 8

visc_scale = 0.2
relax = 0.6
step_size = 0.2
damping = 0.7

f32 = jnp.float32
bf16 = jnp.bfloat16


def from_behind(x, axis, by):
    count = lax.axis_size(axis)
    pairs = [(i, i + by) for i in range(count) if 0 <= i + by < count]
    return lax.ppermute(x, axis, pairs)


def facing_rows(first, last):
    even = lax.axis_index("gx") % 2 == 0
    return jnp.where(even, last, first), jnp.where(even, first, last)


def above_below(pair, other, f):
    a = lax.axis_index("gx")
    near = pair[1 - a % 2, f]
    far = other[f]
    even = a % 2 == 0
    return jnp.where(even, far, near), jnp.where(even, near, far)


def exchange_rows(to_pair, to_other):
    count = lax.axis_size("gx")
    swaps = [(i, i + 1) for i in range(1, count - 1, 2)]
    other = lax.ppermute(to_other, "gx", swaps + [(j, i) for i, j in swaps])
    groups = [[i, i + 1] for i in range(0, count, 2)]
    pair = lax.all_gather(to_pair, "gx", axis_index_groups=groups)
    return pair, other


def iota(shape, dim):
    return lax.broadcasted_iota(jnp.int32, shape, dim)


def split3(x):
    hi = x.astype(bf16).astype(f32)
    rest = x - hi
    mid = rest.astype(bf16).astype(f32)
    return hi, mid, rest - mid


def interleave(parts_u, parts_v):
    return [part for both in zip(parts_u, parts_v) for part in both]


def sum_parts(x):
    return x[0:2] + x[2:4] + x[4:6]


def contract_last(a, b):
    return lax.dot_general(a, b, (((1,), (1,)), ((), ())), preferred_element_type=f32)


def keep_parts(ref, parts):
    for p, part in enumerate(parts):
        ref[ROWS * p : ROWS * p + ROWS, :] = part
    ref[ROWS * len(parts) :, :] = jnp.zeros((ROWS * (8 - len(parts)), COLS), f32)


def parts_of_row(ref, i):
    return ref[pl.ds(i, 8, stride=ROWS), :]


def tile_fields(forcing, strength, mask):
    cover = mask.astype(f32)
    spread = (iota((16, COLS), 1) // 8 == iota((16, COLS), 0)).astype(f32)
    parts = jnp.concatenate(split3(strength), axis=0).astype(bf16)
    wide = jnp.dot(parts, spread.astype(bf16), preferred_element_type=f32)
    wide = (wide[0:4] + wide[4:8]) + wide[8:12]
    fine = jnp.concatenate([jnp.broadcast_to(wide[i : i + 1], (8, COLS)) for i in range(ROWS // 8)], axis=0)
    return forcing[0], forcing[1], cover, visc_scale * fine * cover


def pack_kernel(
    forcing_in, strength_in, mask_in, recv_in, cells_in, codes_in, observed_in,
    out, own, table, observed,
    forcing, strength, mask, recv, sems,
):
    b = lax.axis_index("gy")
    sources = (forcing_in, strength_in, mask_in, recv_in, cells_in, codes_in, observed_in)
    targets = (forcing, strength, mask, recv, table.at[0], table.at[1], observed)
    copies = [pltpu.make_async_copy(a, t, sems.at[i]) for i, (a, t) in enumerate(zip(sources, targets))]
    for copy in copies:
        copy.start()
    for copy in copies:
        copy.wait()
    fields = tile_fields(forcing[...], strength[...], mask[...])
    for f in range(4):
        own[f] = fields[f]
    lane = iota((8, COLS), 1)
    left = jnp.zeros((8, COLS), f32)
    right = jnp.zeros((8, COLS), f32)
    for g in range(4):
        for f in range(4):
            at = 32 * g + 8 * f
            piece = fields[f][8 * g : 8 * g + 8]
            here = (lane >= at) & (lane < at + 8)
            left = jnp.where(here, pltpu.roll(piece, at, 1) if at else piece, left)
            right = jnp.where(here, pltpu.roll(piece, at + 8, 1), right)
    slots = recv[...].astype(f32)
    for d in range(OWNERS):
        out[d, 0:8, :] = jnp.where(d < b, left, right)
        out[d, 8:12, :] = slots[4 * d : 4 * d + 4]


def widen_kernel(received, own, ext, to_pair, to_other):
    b = lax.axis_index("gy")
    lane = iota((8, COLS), 1)
    from_left = received[jnp.maximum(b - 1, 0), 0:8, :] * (b > 0).astype(f32)
    from_right = received[jnp.minimum(b + 1, OWNERS - 1), 0:8, :] * (b < OWNERS - 1).astype(f32)
    for f in range(4):
        ext[f, :, 0:COLS] = own[f]
        for g in range(4):
            at = 32 * g + 8 * f
            low = pltpu.roll(from_right, (COLS - at) % COLS, 1) if at else from_right
            high = pltpu.roll(from_left, (120 - at) % COLS, 1)
            ext[f, 8 * g : 8 * g + 8, COLS:] = jnp.where(lane < 8, low, jnp.where(lane >= 120, high, 0.0))
    to_pair[...], to_other[...] = facing_rows(ext[:, 0:8, :], ext[:, ROWS - 8 : ROWS, :])


def next_row(x):
    return pltpu.roll(x, x.shape[0] - 1, 0)


def prev_row(x):
    return pltpu.roll(x, 1, 0)


def next_col(x):
    return pltpu.roll(x, x.shape[1] - 1, 1)


def prev_col(x):
    return pltpu.roll(x, 1, 1)


def forward_kernel(ext, pair, other, received, table, observed, sums, rates, window, table_out, vel, kept, hot, total, sems):
    b = lax.axis_index("gy")
    slot_ids = iota((COLS, COLS), 0)
    slots = jnp.concatenate([received[d, 8:12, :] for d in range(OWNERS)], axis=0).astype(jnp.int32)
    table_out[0] = table[0]
    table_out[1] = table[1]
    table_out[2] = slots
    for i in range(ROWS):
        at = slice(COLS * i, COLS * i + COLS)
        hot[:, at] = (slot_ids == slots[i : i + 1, :] % COLS).astype(f32).astype(bf16)
    fields = []
    for f in range(4):
        above, below = above_below(pair, other, f)
        fields.append(jnp.concatenate([above, ext[f], below], axis=0))
    force_x, force_y, cover, visc = fields
    window[0] = cover
    window[1] = visc
    tau_x = step_size * cover * force_x
    tau_y = step_size * cover * force_y
    big = (0.625 * step_size) * visc
    small = (0.375 * step_size) * visc
    quarter = (0.25 * step_size) * visc
    big_p, small_p, quarter_p = prev_col(big), prev_col(small), prev_col(quarter)
    u, v = tau_x, tau_y
    nx = ny = s3 = ny_p = s3_p = None
    own = slice(HALO, HALO + ROWS)
    for step in range(SUBCYCLES - 1):
        u_p, v_p = prev_col(u), prev_col(v)
        ex = next_row(u) - u
        ey = next_col(v) - v
        sh = (next_col(u) - u) + (next_row(v) - v)
        ex_p = next_row(u_p) - u_p
        ey_p = v - v_p
        sh_p = (u - u_p) + (next_row(v_p) - v_p)
        rates[step, 0] = ex[own, :COLS]
        rates[step, 1] = ey[own, :COLS]
        rates[step, 2] = sh[own, :COLS]
        dx = big * ex + small * ey
        dy = small * ex + big * ey
        ds = quarter * sh
        dy_p = small_p * ex_p + big_p * ey_p
        ds_p = quarter_p * sh_p
        nx = dx if nx is None else relax * nx + dx
        ny = dy if ny is None else relax * ny + dy
        s3 = ds if s3 is None else relax * s3 + ds
        ny_p = dy_p if ny_p is None else relax * ny_p + dy_p
        s3_p = ds_p if s3_p is None else relax * s3_p + ds_p
        fx = (nx - prev_row(nx)) + (s3 - s3_p)
        fy = (ny - ny_p) + (s3 - prev_row(s3))
        u = damping * u + cover * fx + tau_x
        v = damping * v + cover * fy + tau_y
    vel[0] = u[own, :COLS]
    vel[1] = v[own, :COLS]

    cell = table[0]
    row, col = cell // COLS, cell % COLS
    got_u = jnp.zeros((ROWS, COLS), f32)
    got_v = jnp.zeros((ROWS, COLS), f32)
    for r in range(ROWS):
        hit = row == r
        line_u = jnp.broadcast_to(vel[0, r : r + 1, :], (ROWS, COLS))
        line_v = jnp.broadcast_to(vel[1, r : r + 1, :], (ROWS, COLS))
        got_u = jnp.where(hit, jnp.take_along_axis(line_u, col, axis=1), got_u)
        got_v = jnp.where(hit, jnp.take_along_axis(line_v, col, axis=1), got_v)
    weight = table[1].astype(f32) * (1.0 / 16.0)
    keep_parts(kept, interleave(split3(got_u * weight), split3(got_v * weight)))
    for d in range(OWNERS):
        left = []
        for i in range(4 * d, 4 * d + 4):
            block = parts_of_row(kept, i)
            low = slots[i : i + 1, :] < COLS
            left.append(jnp.concatenate([jnp.where(low, block, 0.0), jnp.where(low, 0.0, block)], axis=0))
        left = jnp.concatenate(left, axis=1).astype(bf16)
        prod = contract_last(left, hot[:, 4 * COLS * d : 4 * COLS * d + 4 * COLS])
        mine = (b == d).astype(f32)
        for h in range(2):
            at = slice(COLS * h, COLS * h + COLS)
            total[2 * d : 2 * d + 2, at] = sum_parts(prod[8 * h : 8 * h + 8]) - mine * observed[:, at]
    copies = [pltpu.make_async_copy(total, sums.at[d], sems.at[d]) for d in range(OWNERS)]
    for copy in copies:
        copy.start()
    for copy in copies:
        copy.wait()


def edge_kernel(own_table, left_table, right_table, col_hot, left_hot, right_hot):
    edge_ids = iota((8 * SPAN, COLS), 0)
    col_ids = iota((COLS, COLS), 0)
    for table, hot, first_col in ((own_table, col_hot, None), (left_table, left_hot, COLS - 8), (right_table, right_hot, 0)):
        cell = table[0]
        weight = table[1].astype(f32) * (1.0 / 16.0)
        row, col = cell // COLS, cell % COLS
        ids, place = col_ids, col
        if first_col is not None:
            ids = edge_ids
            place = jnp.where((col >= first_col) & (col < first_col + 8), row % SPAN * 8 + col % 8, -1)
        for i in range(ROWS):
            at = slice(COLS * i, COLS * i + COLS)
            hot[:, at] = jnp.where(ids == place[i : i + 1, :], weight[i : i + 1, :], 0.0).astype(bf16)


def scatter_kernel(
    sums, left_table, own_table, right_table, col_hot, left_hot, right_hot,
    misfit, adj, to_pair, to_other,
    total, kept, lhs, edge_lhs,
):
    b = lax.axis_index("gy")
    acc = sums[0]
    for j in range(1, OWNERS):
        acc = acc + sums[j]
    total[...] = acc
    mine = acc[0:2]
    for d in range(1, OWNERS):
        mine = jnp.where(b == d, acc[2 * d : 2 * d + 2], mine)
    misfit[...] = mine
    sub = iota((8, COLS), 0)
    lane = iota((8, COLS), 1)
    tables = [
        [
            [
                jnp.where(
                    sub < 4,
                    jnp.broadcast_to(total[4 * q + c : 4 * q + c + 1, h : h + COLS], (8, COLS)),
                    jnp.broadcast_to(total[4 * q + 2 + c : 4 * q + 3 + c, h : h + COLS], (8, COLS)),
                )
                for h in (0, COLS)
            ]
            for c in range(2)
        ]
        for q in range(4)
    ]
    row_ids = iota((ROWS, COLS), 0)
    halo = [None, None, None]
    for k in (0, 2, 1):
        row = (left_table, own_table, right_table)[k][0] // COLS
        values = [[], []]
        for q in range(4):
            slot = (left_table, own_table, right_table)[k][2, 8 * q : 8 * q + 8, :]
            near = slot % COLS
            for c in range(2):
                values[c].append(
                    jnp.where(
                        slot < COLS,
                        jnp.take_along_axis(tables[q][c][0], near, axis=1),
                        jnp.take_along_axis(tables[q][c][1], near, axis=1),
                    )
                )
        parts = interleave(*(split3(jnp.concatenate(values[c], axis=0)) for c in range(2)))
        if k == 1:
            for i in range(ROWS):
                at = slice(COLS * i, COLS * i + COLS)
                hit = row_ids == row[i : i + 1, :]
                for p, part in enumerate(parts):
                    lhs[ROWS * p : ROWS * p + ROWS, at] = jnp.where(hit, part[i : i + 1, :], 0.0).astype(bf16)
            prod = contract_last(lhs[...], col_hot[...])
            for c in range(2):
                adj[c, :, 0:COLS] = sum(prod[ROWS * p : ROWS * p + ROWS] for p in (c, c + 2, c + 4))
        else:
            keep_parts(kept.at[k // 2], parts)
            group = row // SPAN
            for i in range(ROWS):
                block = parts_of_row(kept.at[k // 2], i)
                edge_lhs[:, COLS * i : COLS * i + COLS] = jnp.concatenate(
                    [jnp.where(group[i : i + 1, :] == g, block, 0.0) for g in range(ROWS // SPAN)], axis=0
                ).astype(bf16)
            prod = contract_last(edge_lhs[...], (right_hot if k else left_hot)[...])
            halo[k] = [sum_parts(prod[8 * g : 8 * g + 8]) for g in range(ROWS // SPAN)]
    for c in range(2):
        for q in range(4):
            first_row = 8 * q % SPAN
            where = ((first_row % 16 + sub) * 8 + lane % 8) % COLS
            sides = []
            for k in (2, 0):
                line = halo[k][8 * q // SPAN][c : c + 1]
                line = line[:, 8 * (first_row - first_row % 16) :][:, :COLS]
                if line.shape[1] < COLS:
                    line = jnp.concatenate([line, line], axis=1)
                sides.append(jnp.take_along_axis(jnp.broadcast_to(line, (8, COLS)), where, axis=1))
            adj[c, 8 * q : 8 * q + 8, COLS:] = jnp.where(lane < 8, sides[0], jnp.where(lane >= 120, sides[1], 0.0))
    to_pair[...], to_other[...] = facing_rows(adj[:, 0:8, :], adj[:, ROWS - 8 : ROWS, :])


def adjoint_kernel(adj, pair, other, window, rates, misfit, out, misfit_out, sem):
    copy = pltpu.make_async_copy(misfit, misfit_out, sem.at[0])
    copy.start()
    cover = window[0]
    visc = window[1]
    scaled = step_size * cover
    third = 0.25 * visc
    visc_p, third_p = prev_col(visc), prev_col(third)
    states = []
    for c in range(2):
        above, below = above_below(pair, other, c)
        states.append(scaled * jnp.concatenate([above, adj[c], below], axis=0))
    w0, w1 = states
    own = slice(HALO, HALO + ROWS)
    a = h = t = h_p = t_p = None
    grad = None
    for step in range(SUBCYCLES - 2, -1, -1):
        w0_p, w1_p = prev_col(w0), prev_col(w1)
        ax = w0 - next_row(w0)
        ay = w1 - next_col(w1)
        at = (w0 - next_col(w0)) + (w1 - next_row(w1))
        ax_p = w0_p - next_row(w0_p)
        ay_p = w1_p - w1
        at_p = (w0_p - w0) + (w1_p - next_row(w1_p))
        da = 0.625 * ax + 0.375 * ay
        dh = 0.375 * ax + 0.625 * ay
        dh_p = 0.375 * ax_p + 0.625 * ay_p
        a = da if a is None else relax * a + da
        h = dh if h is None else relax * h + dh
        t = at if t is None else relax * t + at
        h_p = dh_p if h_p is None else relax * h_p + dh_p
        t_p = at_p if t_p is None else relax * t_p + at_p
        term = (
            a[own, :COLS] * rates[step, 0]
            + h[own, :COLS] * rates[step, 1]
            + 0.25 * (t[own, :COLS] * rates[step, 2])
        )
        grad = term if grad is None else grad + term
        if step:
            ra, rh, rt = visc * a, visc * h, third * t
            w0 = damping * w0 + scaled * ((prev_row(ra) - ra) + (third_p * t_p - rt))
            w1 = damping * w1 + scaled * ((visc_p * h_p - rh) + (prev_row(rt) - rt))
    grad = visc_scale * cover[own, :COLS] * grad
    rows = jnp.concatenate(
        [jnp.sum(grad[8 * i : 8 * i + 8], axis=0, keepdims=True) for i in range(ROWS // 8)], axis=0
    )
    gather = (iota((COLS, 16), 0) // 8 == iota((COLS, 16), 1)).astype(f32)
    parts = jnp.concatenate(split3(rows), axis=0).astype(bf16)
    sums = jnp.dot(parts, gather.astype(bf16), preferred_element_type=f32)
    out[...] = sums[0:4] + sums[4:8] + sums[8:12]
    copy.wait()


def call(kernel, outs, args, far=(), scratch=(), cost=0, limit=8):
    far = [pltpu.with_memory_space_constraint(x, pltpu.HBM) for x in far]
    near = pl.BlockSpec(memory_space=pltpu.VMEM)
    return pl.pallas_call(
        kernel,
        out_shape=tuple(outs),
        in_specs=[near] * len(args) + [pl.BlockSpec(memory_space=pltpu.HBM)] * len(far),
        out_specs=tuple(pl.BlockSpec(memory_space=o.memory_space) for o in outs),
        scratch_shapes=list(scratch),
        cost_estimate=pl.CostEstimate(flops=cost, bytes_accessed=0, transcendentals=0) if cost else None,
        compiler_params=pltpu.CompilerParams(vmem_limit_bytes=limit * 1024 * 1024),
    )(*args, *far)


def near(*shape, dtype=f32):
    return pltpu.VMEM(shape, dtype)


def per_device(forcing, strength, mask, send_cell, send_code, recv_buoy, observed):
    forcing = forcing[0]
    cells = send_cell.reshape(ROWS, COLS)
    codes = send_code.reshape(ROWS, COLS)
    recv = recv_buoy.reshape(ROWS, COLS)
    observed = observed.reshape(2, BUOYS)
    entries = ROWS * COLS
    packed, own, table, observed = call(
        pack_kernel,
        [near(OWNERS, 12, COLS), near(4, ROWS, COLS), near(2, ROWS, COLS, dtype=jnp.int32), near(2, BUOYS)],
        (),
        (forcing, strength, mask, recv, cells, codes, observed),
        [
            near(2, ROWS, COLS),
            near(ROWS // 8, COLS // 8),
            near(ROWS, COLS, dtype=jnp.int32),
            near(ROWS, COLS, dtype=jnp.int32),
            pltpu.SemaphoreType.DMA((7,)),
        ],
    )
    received = lax.all_to_all(packed, "gy", 0, 0, tiled=True)
    ext, to_pair, to_other = call(
        widen_kernel,
        [near(4, ROWS, 2 * COLS), near(4, 8, 2 * COLS), near(4, 8, 2 * COLS)],
        (received, own),
    )
    pair, other = exchange_rows(to_pair, to_other)
    sums, rates, window, table = call(
        forward_kernel,
        [
            pltpu.HBM((OWNERS, 2 * OWNERS, BUOYS), f32),
            near(SUBCYCLES - 1, 3, ROWS, COLS),
            near(2, WIN, 2 * COLS),
            near(3, ROWS, COLS, dtype=jnp.int32),
        ],
        (ext, pair, other, received, table, observed),
        (),
        [
            near(2, ROWS, COLS),
            near(8 * ROWS, COLS),
            near(COLS, entries, dtype=bf16),
            near(2 * OWNERS, BUOYS),
            pltpu.SemaphoreType.DMA((OWNERS,)),
        ],
    )
    sums = lax.all_to_all(sums, "gy", 0, 0, tiled=True)
    left_table = from_behind(table, "gy", 1)
    right_table = from_behind(table, "gy", -1)
    col_hot, left_hot, right_hot = call(
        edge_kernel,
        [near(COLS, entries, dtype=bf16), near(8 * SPAN, entries, dtype=bf16), near(8 * SPAN, entries, dtype=bf16)],
        (table, left_table, right_table),
        cost=10**9,
    )
    misfit, adj, to_pair, to_other = call(
        scatter_kernel,
        [
            near(2, BUOYS),
            near(2, ROWS, 2 * COLS),
            near(2, 8, 2 * COLS),
            near(2, 8, 2 * COLS),
        ],
        (sums, left_table, table, right_table, col_hot, left_hot, right_hot),
        (),
        [
            near(2 * OWNERS, BUOYS),
            near(2, 8 * ROWS, COLS),
            near(6 * ROWS, entries, dtype=bf16),
            near(8 * ROWS // SPAN, entries, dtype=bf16),
        ],
    )
    pair, other = exchange_rows(to_pair, to_other)
    coarse, misfit = call(
        adjoint_kernel,
        [near(ROWS // 8, COLS // 8), pltpu.HBM((2, BUOYS), f32)],
        (adj, pair, other, window, rates, misfit),
        (),
        [pltpu.SemaphoreType.DMA((1,))],
    )
    gradient = jnp.sum(lax.all_gather(coarse, "member"), axis=0)
    return (misfit[None, None, None], gradient)


def solution(mesh):
    return jax.shard_map(
        per_device,
        mesh=mesh,
        in_specs=(
            P("member", None, "gx", "gy"),
            P("gx", "gy"),
            P("gx", "gy"),
            P("member", "gx", "gy", None),
            P("member", "gx", "gy", None),
            P("member", "gx", "gy", None),
            P("member", "gx", "gy", None, None),
        ),
        out_specs=(P("member", "gx", "gy", None, None), P("gx", "gy")),
        check_vma=False,
    )
```

```python
import jax
import jax.numpy as jnp
from jax import lax
from jax.experimental import pallas as pl
from jax.experimental.pallas import tpu as pltpu
from jax.sharding import PartitionSpec as P

SUBCYCLES = 8
BUOYS = 256
HALO = 8
ROWS = 32
COLS = 128
WIN = ROWS + 2 * HALO
OWNERS = 8
SPAN = 8

visc_scale = 0.2
relax = 0.6
step_size = 0.2
damping = 0.7

f32 = jnp.float32
bf16 = jnp.bfloat16


def from_behind(x, axis, by):
    count = lax.axis_size(axis)
    pairs = [(i, i + by) for i in range(count) if 0 <= i + by < count]
    return lax.ppermute(x, axis, pairs)


def facing_rows(first, last):
    even = lax.axis_index("gx") % 2 == 0
    return jnp.where(even, last, first), jnp.where(even, first, last)


def above_below(pair, other, f):
    a = lax.axis_index("gx")
    near = pair[1 - a % 2, f]
    far = other[f]
    even = a % 2 == 0
    return jnp.where(even, far, near), jnp.where(even, near, far)


def exchange_rows(to_pair, to_other):
    count = lax.axis_size("gx")
    swaps = [(i, i + 1) for i in range(1, count - 1, 2)]
    other = lax.ppermute(to_other, "gx", swaps + [(j, i) for i, j in swaps])
    groups = [[i, i + 1] for i in range(0, count, 2)]
    pair = lax.all_gather(to_pair, "gx", axis_index_groups=groups)
    return pair, other


def iota(shape, dim):
    return lax.broadcasted_iota(jnp.int32, shape, dim)


def split3(x):
    hi = x.astype(bf16).astype(f32)
    rest = x - hi
    mid = rest.astype(bf16).astype(f32)
    return hi, mid, rest - mid


def interleave(parts_u, parts_v):
    return [part for both in zip(parts_u, parts_v) for part in both]


def sum_parts(x):
    return x[0:2] + x[2:4] + x[4:6]


def contract_last(a, b):
    return lax.dot_general(a, b, (((1,), (1,)), ((), ())), preferred_element_type=f32)


def keep_parts(ref, parts):
    for p, part in enumerate(parts):
        ref[ROWS * p : ROWS * p + ROWS, :] = part
    ref[ROWS * len(parts) :, :] = jnp.zeros((ROWS * (8 - len(parts)), COLS), f32)


def parts_of_row(ref, i):
    return ref[pl.ds(i, 8, stride=ROWS), :]


def tile_fields(forcing, strength, mask):
    cover = mask.astype(f32)
    spread = (iota((16, COLS), 1) // 8 == iota((16, COLS), 0)).astype(f32)
    parts = jnp.concatenate(split3(strength), axis=0).astype(bf16)
    wide = jnp.dot(parts, spread.astype(bf16), preferred_element_type=f32)
    wide = (wide[0:4] + wide[4:8]) + wide[8:12]
    fine = jnp.concatenate([jnp.broadcast_to(wide[i : i + 1], (8, COLS)) for i in range(ROWS // 8)], axis=0)
    return forcing[0], forcing[1], cover, visc_scale * fine * cover


def pack_kernel(
    forcing_in, strength_in, mask_in, recv_in, cells_in, codes_in, observed_in,
    out, own, table, observed,
    forcing, strength, mask, recv, sems,
):
    b = lax.axis_index("gy")
    sources = (forcing_in, strength_in, mask_in, recv_in, cells_in, codes_in, observed_in)
    targets = (forcing, strength, mask, recv, table.at[0], table.at[1], observed)
    copies = [pltpu.make_async_copy(a, t, sems.at[i]) for i, (a, t) in enumerate(zip(sources, targets))]
    for copy in copies:
        copy.start()
    for copy in copies:
        copy.wait()
    fields = tile_fields(forcing[...], strength[...], mask[...])
    for f in range(4):
        own[f] = fields[f]
    lane = iota((8, COLS), 1)
    left = jnp.zeros((8, COLS), f32)
    right = jnp.zeros((8, COLS), f32)
    for g in range(4):
        for f in range(4):
            at = 32 * g + 8 * f
            piece = fields[f][8 * g : 8 * g + 8]
            here = (lane >= at) & (lane < at + 8)
            left = jnp.where(here, pltpu.roll(piece, at, 1) if at else piece, left)
            right = jnp.where(here, pltpu.roll(piece, at + 8, 1), right)
    slots = recv[...].astype(f32)
    for d in range(OWNERS):
        strip = jnp.where(d < b, left, right)
        out[d, 0] = strip[0:4]
        out[d, 1] = strip[4:8]
        out[d, 2] = slots[4 * d : 4 * d + 4]


def widen_kernel(received, own, ext, to_pair, to_other):
    b = lax.axis_index("gy")
    lane = iota((8, COLS), 1)
    left, right = jnp.maximum(b - 1, 0), jnp.minimum(b + 1, OWNERS - 1)
    from_left = jnp.concatenate([received[left, n] for n in range(2)], axis=0) * (b > 0).astype(f32)
    from_right = jnp.concatenate([received[right, n] for n in range(2)], axis=0) * (b < OWNERS - 1).astype(f32)
    for f in range(4):
        ext[f, :, 0:COLS] = own[f]
        for g in range(4):
            at = 32 * g + 8 * f
            low = pltpu.roll(from_right, (COLS - at) % COLS, 1) if at else from_right
            high = pltpu.roll(from_left, (120 - at) % COLS, 1)
            ext[f, 8 * g : 8 * g + 8, COLS:] = jnp.where(lane < 8, low, jnp.where(lane >= 120, high, 0.0))
    to_pair[...], to_other[...] = facing_rows(ext[:, 0:8, :], ext[:, ROWS - 8 : ROWS, :])


def next_row(x):
    return pltpu.roll(x, x.shape[0] - 1, 0)


def prev_row(x):
    return pltpu.roll(x, 1, 0)


def next_col(x):
    return pltpu.roll(x, x.shape[1] - 1, 1)


def prev_col(x):
    return pltpu.roll(x, 1, 1)


def forward_kernel(ext, pair, other, received, table, observed, sums, rates, window, table_out, vel, kept, hot, total, sems):
    b = lax.axis_index("gy")
    slot_ids = iota((COLS, COLS), 0)
    slots = jnp.concatenate([received[d, 2] for d in range(OWNERS)], axis=0).astype(jnp.int32)
    table_out[0] = table[0]
    table_out[1] = table[1]
    table_out[2] = slots
    for i in range(ROWS):
        at = slice(COLS * i, COLS * i + COLS)
        hot[:, at] = (slot_ids == slots[i : i + 1, :] % COLS).astype(f32).astype(bf16)
    fields = []
    for f in range(4):
        above, below = above_below(pair, other, f)
        fields.append(jnp.concatenate([above, ext[f], below], axis=0))
    force_x, force_y, cover, visc = fields
    window[0] = cover
    window[1] = visc
    tau_x = step_size * cover * force_x
    tau_y = step_size * cover * force_y
    big = (0.625 * step_size) * visc
    small = (0.375 * step_size) * visc
    quarter = (0.25 * step_size) * visc
    visc_p = prev_col(visc)
    big_p, small_p, quarter_p = ((c * step_size) * visc_p for c in (0.625, 0.375, 0.25))
    u, v = tau_x, tau_y
    nx = ny = s3 = ny_p = s3_p = None
    own = slice(HALO, HALO + ROWS)
    for step in range(SUBCYCLES - 1):
        u_p, v_p = prev_col(u), prev_col(v)
        ex = next_row(u) - u
        ey = next_col(v) - v
        sh = (next_col(u) - u) + (next_row(v) - v)
        ex_p = next_row(u_p) - u_p
        ey_p = v - v_p
        sh_p = (u - u_p) + (next_row(v_p) - v_p)
        rates[step, 0] = ex[own, :COLS]
        rates[step, 1] = ey[own, :COLS]
        rates[step, 2] = sh[own, :COLS]
        dx = big * ex + small * ey
        dy = small * ex + big * ey
        ds = quarter * sh
        dy_p = small_p * ex_p + big_p * ey_p
        ds_p = quarter_p * sh_p
        nx = dx if nx is None else relax * nx + dx
        ny = dy if ny is None else relax * ny + dy
        s3 = ds if s3 is None else relax * s3 + ds
        ny_p = dy_p if ny_p is None else relax * ny_p + dy_p
        s3_p = ds_p if s3_p is None else relax * s3_p + ds_p
        fx = (nx - prev_row(nx)) + (s3 - s3_p)
        fy = (ny - ny_p) + (s3 - prev_row(s3))
        u = damping * u + cover * fx + tau_x
        v = damping * v + cover * fy + tau_y
    vel[0] = u[own, :COLS]
    vel[1] = v[own, :COLS]

    cell = table[0]
    row, col = cell // COLS, cell % COLS
    got_u = jnp.zeros((ROWS, COLS), f32)
    got_v = jnp.zeros((ROWS, COLS), f32)
    for r in range(ROWS):
        hit = row == r
        line_u = jnp.broadcast_to(vel[0, r : r + 1, :], (ROWS, COLS))
        line_v = jnp.broadcast_to(vel[1, r : r + 1, :], (ROWS, COLS))
        got_u = jnp.where(hit, jnp.take_along_axis(line_u, col, axis=1), got_u)
        got_v = jnp.where(hit, jnp.take_along_axis(line_v, col, axis=1), got_v)
    weight = table[1].astype(f32) * (1.0 / 16.0)
    keep_parts(kept, interleave(split3(got_u * weight), split3(got_v * weight)))
    for d in range(OWNERS):
        left = []
        for i in range(4 * d, 4 * d + 4):
            block = parts_of_row(kept, i)
            low = slots[i : i + 1, :] < COLS
            left.append(jnp.concatenate([jnp.where(low, block, 0.0), jnp.where(low, 0.0, block)], axis=0))
        left = jnp.concatenate(left, axis=1).astype(bf16)
        prod = contract_last(left, hot[:, 4 * COLS * d : 4 * COLS * d + 4 * COLS])
        mine = (b == d).astype(f32)
        for h in range(2):
            at = slice(COLS * h, COLS * h + COLS)
            total[2 * d : 2 * d + 2, at] = sum_parts(prod[8 * h : 8 * h + 8]) - mine * observed[:, at]
    copies = [pltpu.make_async_copy(total, sums.at[d], sems.at[d]) for d in range(OWNERS)]
    for copy in copies:
        copy.start()
    for copy in copies:
        copy.wait()


def edge_kernel(own_table, left_table, right_table, col_hot, left_hot, right_hot):
    edge_ids = iota((8 * SPAN, COLS), 0)
    col_ids = iota((COLS, COLS), 0)
    for table, hot, first_col in ((own_table, col_hot, None), (left_table, left_hot, COLS - 8), (right_table, right_hot, 0)):
        cell = table[0]
        weight = table[1].astype(f32) * (1.0 / 16.0)
        row, col = cell // COLS, cell % COLS
        ids, place = col_ids, col
        if first_col is not None:
            ids = edge_ids
            place = jnp.where((col >= first_col) & (col < first_col + 8), row % SPAN * 8 + col % 8, -1)
        for i in range(ROWS):
            at = slice(COLS * i, COLS * i + COLS)
            hot[:, at] = jnp.where(ids == place[i : i + 1, :], weight[i : i + 1, :], 0.0).astype(bf16)


def scatter_kernel(
    sums, left_table, own_table, right_table, col_hot, left_hot, right_hot,
    misfit, adj, to_pair, to_other,
    total, kept, lhs, edge_lhs,
):
    b = lax.axis_index("gy")
    acc = sums[0]
    for j in range(1, OWNERS):
        acc = acc + sums[j]
    total[...] = acc
    mine = acc[0:2]
    for d in range(1, OWNERS):
        mine = jnp.where(b == d, acc[2 * d : 2 * d + 2], mine)
    misfit[...] = mine
    sub = iota((8, COLS), 0)
    lane = iota((8, COLS), 1)
    tables = [
        [
            [
                jnp.where(
                    sub < 4,
                    jnp.broadcast_to(total[4 * q + c : 4 * q + c + 1, h : h + COLS], (8, COLS)),
                    jnp.broadcast_to(total[4 * q + 2 + c : 4 * q + 3 + c, h : h + COLS], (8, COLS)),
                )
                for h in (0, COLS)
            ]
            for c in range(2)
        ]
        for q in range(4)
    ]
    row_ids = iota((ROWS, COLS), 0)
    halo = [None, None, None]
    for k in (0, 2, 1):
        row = (left_table, own_table, right_table)[k][0] // COLS
        values = [[], []]
        for q in range(4):
            slot = (left_table, own_table, right_table)[k][2, 8 * q : 8 * q + 8, :]
            near = slot % COLS
            for c in range(2):
                values[c].append(
                    jnp.where(
                        slot < COLS,
                        jnp.take_along_axis(tables[q][c][0], near, axis=1),
                        jnp.take_along_axis(tables[q][c][1], near, axis=1),
                    )
                )
        parts = interleave(*(split3(jnp.concatenate(values[c], axis=0)) for c in range(2)))
        if k == 1:
            for i in range(ROWS):
                at = slice(COLS * i, COLS * i + COLS)
                hit = row_ids == row[i : i + 1, :]
                for p, part in enumerate(parts):
                    lhs[ROWS * p : ROWS * p + ROWS, at] = jnp.where(hit, part[i : i + 1, :], 0.0).astype(bf16)
            prod = contract_last(lhs[...], col_hot[...])
            for c in range(2):
                adj[c, :, 0:COLS] = sum(prod[ROWS * p : ROWS * p + ROWS] for p in (c, c + 2, c + 4))
        else:
            keep_parts(kept.at[k // 2], parts)
            group = row // SPAN
            for i in range(ROWS):
                block = parts_of_row(kept.at[k // 2], i)
                edge_lhs[:, COLS * i : COLS * i + COLS] = jnp.concatenate(
                    [jnp.where(group[i : i + 1, :] == g, block, 0.0) for g in range(ROWS // SPAN)], axis=0
                ).astype(bf16)
            prod = contract_last(edge_lhs[...], (right_hot if k else left_hot)[...])
            halo[k] = [sum_parts(prod[8 * g : 8 * g + 8]) for g in range(ROWS // SPAN)]
    for c in range(2):
        for q in range(4):
            first_row = 8 * q % SPAN
            where = ((first_row % 16 + sub) * 8 + lane % 8) % COLS
            sides = []
            for k in (2, 0):
                line = halo[k][8 * q // SPAN][c : c + 1]
                line = line[:, 8 * (first_row - first_row % 16) :][:, :COLS]
                if line.shape[1] < COLS:
                    line = jnp.concatenate([line, line], axis=1)
                sides.append(jnp.take_along_axis(jnp.broadcast_to(line, (8, COLS)), where, axis=1))
            adj[c, 8 * q : 8 * q + 8, COLS:] = jnp.where(lane < 8, sides[0], jnp.where(lane >= 120, sides[1], 0.0))
    to_pair[...], to_other[...] = facing_rows(adj[:, 0:8, :], adj[:, ROWS - 8 : ROWS, :])


def adjoint_kernel(adj, pair, other, window, rates, misfit, out, misfit_out, sem):
    copy = pltpu.make_async_copy(misfit, misfit_out, sem.at[0])
    copy.start()
    cover = window[0]
    visc = window[1]
    scaled = step_size * cover
    third = 0.25 * visc
    visc_p = prev_col(visc)
    third_p = 0.25 * visc_p
    states = []
    for c in range(2):
        above, below = above_below(pair, other, c)
        states.append(scaled * jnp.concatenate([above, adj[c], below], axis=0))
    w0, w1 = states
    own = slice(HALO, HALO + ROWS)
    a = h = t = h_p = t_p = None
    grad = None
    for step in range(SUBCYCLES - 2, -1, -1):
        w0_p, w1_p = prev_col(w0), prev_col(w1)
        ax = w0 - next_row(w0)
        ay = w1 - next_col(w1)
        at = (w0 - next_col(w0)) + (w1 - next_row(w1))
        ax_p = w0_p - next_row(w0_p)
        ay_p = w1_p - w1
        at_p = (w0_p - w0) + (w1_p - next_row(w1_p))
        da = 0.625 * ax + 0.375 * ay
        dh = 0.375 * ax + 0.625 * ay
        dh_p = 0.375 * ax_p + 0.625 * ay_p
        a = da if a is None else relax * a + da
        h = dh if h is None else relax * h + dh
        t = at if t is None else relax * t + at
        h_p = dh_p if h_p is None else relax * h_p + dh_p
        t_p = at_p if t_p is None else relax * t_p + at_p
        term = (
            a[own, :COLS] * rates[step, 0]
            + h[own, :COLS] * rates[step, 1]
            + 0.25 * (t[own, :COLS] * rates[step, 2])
        )
        grad = term if grad is None else grad + term
        if step:
            ra, rh, rt = visc * a, visc * h, third * t
            w0 = damping * w0 + scaled * ((prev_row(ra) - ra) + (third_p * t_p - rt))
            w1 = damping * w1 + scaled * ((visc_p * h_p - rh) + (prev_row(rt) - rt))
    grad = visc_scale * cover[own, :COLS] * grad
    rows = jnp.concatenate(
        [jnp.sum(grad[8 * i : 8 * i + 8], axis=0, keepdims=True) for i in range(ROWS // 8)], axis=0
    )
    gather = (iota((COLS, 16), 0) // 8 == iota((COLS, 16), 1)).astype(f32)
    parts = jnp.concatenate(split3(rows), axis=0).astype(bf16)
    sums = jnp.dot(parts, gather.astype(bf16), preferred_element_type=f32)
    out[...] = sums[0:4] + sums[4:8] + sums[8:12]
    copy.wait()


def call(kernel, outs, args, far=(), scratch=(), cost=0, limit=8):
    far = [pltpu.with_memory_space_constraint(x, pltpu.HBM) for x in far]
    near = pl.BlockSpec(memory_space=pltpu.VMEM)
    return pl.pallas_call(
        kernel,
        out_shape=tuple(outs),
        in_specs=[near] * len(args) + [pl.BlockSpec(memory_space=pltpu.HBM)] * len(far),
        out_specs=tuple(pl.BlockSpec(memory_space=o.memory_space) for o in outs),
        scratch_shapes=list(scratch),
        cost_estimate=pl.CostEstimate(flops=cost, bytes_accessed=0, transcendentals=0) if cost else None,
        compiler_params=pltpu.CompilerParams(vmem_limit_bytes=limit * 1024 * 1024),
    )(*args, *far)


def near(*shape, dtype=f32):
    return pltpu.VMEM(shape, dtype)


def per_device(forcing, strength, mask, send_cell, send_code, recv_buoy, observed):
    forcing = forcing[0]
    cells = send_cell.reshape(ROWS, COLS)
    codes = send_code.reshape(ROWS, COLS)
    recv = recv_buoy.reshape(ROWS, COLS)
    observed = observed.reshape(2, BUOYS)
    entries = ROWS * COLS
    packed, own, table, observed = call(
        pack_kernel,
        [near(OWNERS, 3, 4, COLS), near(4, ROWS, COLS), near(2, ROWS, COLS, dtype=jnp.int32), near(2, BUOYS)],
        (),
        (forcing, strength, mask, recv, cells, codes, observed),
        [
            near(2, ROWS, COLS),
            near(ROWS // 8, COLS // 8),
            near(ROWS, COLS, dtype=jnp.int32),
            near(ROWS, COLS, dtype=jnp.int32),
            pltpu.SemaphoreType.DMA((7,)),
        ],
    )
    received = lax.all_to_all(packed, "gy", 0, 0, tiled=True)
    ext, to_pair, to_other = call(
        widen_kernel,
        [near(4, ROWS, 2 * COLS), near(4, 8, 2 * COLS), near(4, 8, 2 * COLS)],
        (received, own),
    )
    pair, other = exchange_rows(to_pair, to_other)
    sums, rates, window, table = call(
        forward_kernel,
        [
            pltpu.HBM((OWNERS, 2 * OWNERS, BUOYS), f32),
            near(SUBCYCLES - 1, 3, ROWS, COLS),
            near(2, WIN, 2 * COLS),
            near(3, ROWS, COLS, dtype=jnp.int32),
        ],
        (ext, pair, other, received, table, observed),
        (),
        [
            near(2, ROWS, COLS),
            near(8 * ROWS, COLS),
            near(COLS, entries, dtype=bf16),
            near(2 * OWNERS, BUOYS),
            pltpu.SemaphoreType.DMA((OWNERS,)),
        ],
    )
    sums = lax.all_to_all(sums, "gy", 0, 0, tiled=True)
    left_table = from_behind(table, "gy", 1)
    right_table = from_behind(table, "gy", -1)
    col_hot, left_hot, right_hot = call(
        edge_kernel,
        [near(COLS, entries, dtype=bf16), near(8 * SPAN, entries, dtype=bf16), near(8 * SPAN, entries, dtype=bf16)],
        (table, left_table, right_table),
        cost=10**9,
    )
    misfit, adj, to_pair, to_other = call(
        scatter_kernel,
        [
            near(2, BUOYS),
            near(2, ROWS, 2 * COLS),
            near(2, 8, 2 * COLS),
            near(2, 8, 2 * COLS),
        ],
        (sums, left_table, table, right_table, col_hot, left_hot, right_hot),
        (),
        [
            near(2 * OWNERS, BUOYS),
            near(2, 8 * ROWS, COLS),
            near(6 * ROWS, entries, dtype=bf16),
            near(8 * ROWS // SPAN, entries, dtype=bf16),
        ],
    )
    pair, other = exchange_rows(to_pair, to_other)
    coarse, misfit = call(
        adjoint_kernel,
        [near(ROWS // 8, COLS // 8), pltpu.HBM((2, BUOYS), f32)],
        (adj, pair, other, window, rates, misfit),
        (),
        [pltpu.SemaphoreType.DMA((1,))],
    )
    gradient = jnp.sum(lax.all_gather(coarse, "member"), axis=0)
    return (misfit[None, None, None], gradient)


def solution(mesh):
    return jax.shard_map(
        per_device,
        mesh=mesh,
        in_specs=(
            P("member", None, "gx", "gy"),
            P("gx", "gy"),
            P("gx", "gy"),
            P("member", "gx", "gy", None),
            P("member", "gx", "gy", None),
            P("member", "gx", "gy", None),
            P("member", "gx", "gy", None, None),
        ),
        out_specs=(P("member", "gx", "gy", None, None), P("gx", "gy")),
        check_vma=False,
    )
```

```python
import jax
import jax.numpy as jnp
from jax import lax
from jax.experimental import pallas as pl
from jax.experimental.pallas import tpu as pltpu
from jax.sharding import PartitionSpec as P

SUBCYCLES = 8
BUOYS = 256
HALO = 8
ROWS = 32
COLS = 128
WIN = ROWS + 2 * HALO
OWNERS = 8
SPAN = 8

visc_scale = 0.2
relax = 0.6
step_size = 0.2
damping = 0.7

f32 = jnp.float32
bf16 = jnp.bfloat16


def from_behind(x, axis, by):
    count = lax.axis_size(axis)
    pairs = [(i, i + by) for i in range(count) if 0 <= i + by < count]
    return lax.ppermute(x, axis, pairs)


def facing_rows(first, last):
    even = lax.axis_index("gx") % 2 == 0
    return jnp.where(even, last, first), jnp.where(even, first, last)


def above_below(pair, other, f):
    a = lax.axis_index("gx")
    near = pair[1 - a % 2, f]
    far = other[f]
    even = a % 2 == 0
    return jnp.where(even, far, near), jnp.where(even, near, far)


def exchange_rows(to_pair, to_other):
    count = lax.axis_size("gx")
    swaps = [(i, i + 1) for i in range(1, count - 1, 2)]
    other = lax.ppermute(to_other, "gx", swaps + [(j, i) for i, j in swaps])
    groups = [[i, i + 1] for i in range(0, count, 2)]
    pair = lax.all_gather(to_pair, "gx", axis_index_groups=groups)
    return pair, other


def iota(shape, dim):
    return lax.broadcasted_iota(jnp.int32, shape, dim)


def split3(x):
    hi = x.astype(bf16).astype(f32)
    rest = x - hi
    mid = rest.astype(bf16).astype(f32)
    return hi, mid, rest - mid


def interleave(parts_u, parts_v):
    return [part for both in zip(parts_u, parts_v) for part in both]


def sum_parts(x):
    return x[0:2] + x[2:4] + x[4:6]


def contract_last(a, b):
    return lax.dot_general(a, b, (((1,), (1,)), ((), ())), preferred_element_type=f32)


def keep_parts(ref, parts):
    for p, part in enumerate(parts):
        ref[ROWS * p : ROWS * p + ROWS, :] = part
    ref[ROWS * len(parts) :, :] = jnp.zeros((ROWS * (8 - len(parts)), COLS), f32)


def parts_of_row(ref, i):
    return ref[pl.ds(i, 8, stride=ROWS), :]


def tile_fields(forcing, strength, mask):
    cover = mask.astype(f32)
    cells_y = COLS // 8
    padded = jnp.concatenate([strength, jnp.zeros((ROWS // 8, COLS - cells_y), f32)], axis=1)
    padded = jnp.concatenate([padded, padded], axis=0)
    wide = jnp.take_along_axis(padded, iota((8, COLS), 1) // 8, axis=1)
    fine = jnp.concatenate([jnp.broadcast_to(wide[i : i + 1], (8, COLS)) for i in range(ROWS // 8)], axis=0)
    return forcing[0], forcing[1], cover, visc_scale * fine * cover


def pack_kernel(
    forcing_in, strength_in, mask_in, recv_in, cells_in, codes_in, observed_in,
    out, own, table, observed,
    forcing, strength, mask, recv, sems,
):
    b = lax.axis_index("gy")
    sources = (forcing_in, strength_in, mask_in, recv_in, cells_in, codes_in, observed_in)
    targets = (forcing, strength, mask, recv, table.at[0], table.at[1], observed)
    copies = [pltpu.make_async_copy(a, t, sems.at[i]) for i, (a, t) in enumerate(zip(sources, targets))]
    for copy in copies:
        copy.start()
    for copy in copies[:3]:
        copy.wait()
    fields = tile_fields(forcing[...], strength[...], mask[...])
    for f in range(4):
        own[f] = fields[f]
    lane = iota((8, COLS), 1)
    left = jnp.zeros((8, COLS), f32)
    right = jnp.zeros((8, COLS), f32)
    for g in range(4):
        for f in range(4):
            at = 32 * g + 8 * f
            piece = fields[f][8 * g : 8 * g + 8]
            here = (lane >= at) & (lane < at + 8)
            left = jnp.where(here, pltpu.roll(piece, at, 1) if at else piece, left)
            right = jnp.where(here, pltpu.roll(piece, at + 8, 1), right)
    for copy in copies[3:]:
        copy.wait()
    slots = recv[...].astype(f32)
    for d in range(OWNERS):
        strip = jnp.where(d < b, left, right)
        out[d, 0] = strip[0:4]
        out[d, 1] = strip[4:8]
        out[d, 2] = slots[4 * d : 4 * d + 4]


def widen_kernel(received, own, ext, to_pair, to_other):
    b = lax.axis_index("gy")
    lane = iota((8, COLS), 1)
    left, right = jnp.maximum(b - 1, 0), jnp.minimum(b + 1, OWNERS - 1)
    from_left = jnp.concatenate([received[left, n] for n in range(2)], axis=0) * (b > 0).astype(f32)
    from_right = jnp.concatenate([received[right, n] for n in range(2)], axis=0) * (b < OWNERS - 1).astype(f32)
    for f in range(4):
        ext[f, :, 0:COLS] = own[f]
        for g in range(4):
            at = 32 * g + 8 * f
            low = pltpu.roll(from_right, (COLS - at) % COLS, 1) if at else from_right
            high = pltpu.roll(from_left, (120 - at) % COLS, 1)
            ext[f, 8 * g : 8 * g + 8, COLS:] = jnp.where(lane < 8, low, jnp.where(lane >= 120, high, 0.0))
    to_pair[...], to_other[...] = facing_rows(ext[:, 0:8, :], ext[:, ROWS - 8 : ROWS, :])


def next_row(x):
    return pltpu.roll(x, x.shape[0] - 1, 0)


def prev_row(x):
    return pltpu.roll(x, 1, 0)


def next_col(x):
    return pltpu.roll(x, x.shape[1] - 1, 1)


def prev_col(x):
    return pltpu.roll(x, 1, 1)


def forward_kernel(ext, pair, other, received, table, observed, sums, rates, window, table_out, vel, kept, hot, total, sems):
    b = lax.axis_index("gy")
    slot_ids = iota((COLS, COLS), 0)
    slots = jnp.concatenate([received[d, 2] for d in range(OWNERS)], axis=0).astype(jnp.int32)
    table_out[0] = table[0]
    table_out[1] = table[1]
    table_out[2] = slots
    for i in range(ROWS):
        at = slice(COLS * i, COLS * i + COLS)
        hot[:, at] = (slot_ids == slots[i : i + 1, :] % COLS).astype(f32).astype(bf16)
    fields = []
    for f in range(4):
        above, below = above_below(pair, other, f)
        fields.append(jnp.concatenate([above, ext[f], below], axis=0))
    force_x, force_y, cover, visc = fields
    window[0] = cover
    window[1] = visc
    tau_x = step_size * cover * force_x
    tau_y = step_size * cover * force_y
    big = (0.625 * step_size) * visc
    small = (0.375 * step_size) * visc
    quarter = (0.25 * step_size) * visc
    visc_p = prev_col(visc)
    big_p, small_p, quarter_p = ((c * step_size) * visc_p for c in (0.625, 0.375, 0.25))
    u, v = tau_x, tau_y
    nx = ny = s3 = ny_p = s3_p = None
    own = slice(HALO, HALO + ROWS)
    for step in range(SUBCYCLES - 1):
        u_p, v_p = prev_col(u), prev_col(v)
        ex = next_row(u) - u
        ey = next_col(v) - v
        sh = (next_col(u) - u) + (next_row(v) - v)
        ex_p = next_row(u_p) - u_p
        ey_p = v - v_p
        sh_p = (u - u_p) + (next_row(v_p) - v_p)
        rates[step, 0] = ex[own, :COLS]
        rates[step, 1] = ey[own, :COLS]
        rates[step, 2] = sh[own, :COLS]
        dx = big * ex + small * ey
        dy = small * ex + big * ey
        ds = quarter * sh
        dy_p = small_p * ex_p + big_p * ey_p
        ds_p = quarter_p * sh_p
        nx = dx if nx is None else relax * nx + dx
        ny = dy if ny is None else relax * ny + dy
        s3 = ds if s3 is None else relax * s3 + ds
        ny_p = dy_p if ny_p is None else relax * ny_p + dy_p
        s3_p = ds_p if s3_p is None else relax * s3_p + ds_p
        fx = (nx - prev_row(nx)) + (s3 - s3_p)
        fy = (ny - ny_p) + (s3 - prev_row(s3))
        u = damping * u + cover * fx + tau_x
        v = damping * v + cover * fy + tau_y
    vel[0] = u[own, :COLS]
    vel[1] = v[own, :COLS]

    cell = table[0]
    row, col = cell // COLS, cell % COLS
    got_u = jnp.zeros((ROWS, COLS), f32)
    got_v = jnp.zeros((ROWS, COLS), f32)
    for r in range(ROWS):
        hit = row == r
        line_u = jnp.broadcast_to(vel[0, r : r + 1, :], (ROWS, COLS))
        line_v = jnp.broadcast_to(vel[1, r : r + 1, :], (ROWS, COLS))
        got_u = jnp.where(hit, jnp.take_along_axis(line_u, col, axis=1), got_u)
        got_v = jnp.where(hit, jnp.take_along_axis(line_v, col, axis=1), got_v)
    weight = table[1].astype(f32) * (1.0 / 16.0)
    keep_parts(kept, interleave(split3(got_u * weight), split3(got_v * weight)))
    for d in range(OWNERS):
        left = []
        for i in range(4 * d, 4 * d + 4):
            block = parts_of_row(kept, i)
            low = slots[i : i + 1, :] < COLS
            left.append(jnp.concatenate([jnp.where(low, block, 0.0), jnp.where(low, 0.0, block)], axis=0))
        left = jnp.concatenate(left, axis=1).astype(bf16)
        prod = contract_last(left, hot[:, 4 * COLS * d : 4 * COLS * d + 4 * COLS])
        mine = (b == d).astype(f32)
        for h in range(2):
            at = slice(COLS * h, COLS * h + COLS)
            total[2 * d : 2 * d + 2, at] = sum_parts(prod[8 * h : 8 * h + 8]) - mine * observed[:, at]
    copies = [pltpu.make_async_copy(total, sums.at[d], sems.at[d]) for d in range(OWNERS)]
    for copy in copies:
        copy.start()
    for copy in copies:
        copy.wait()


def edge_kernel(own_table, left_table, right_table, col_hot, left_hot, right_hot):
    edge_ids = iota((8 * SPAN, COLS), 0)
    col_ids = iota((COLS, COLS), 0)
    for table, hot, first_col in ((own_table, col_hot, None), (left_table, left_hot, COLS - 8), (right_table, right_hot, 0)):
        cell = table[0]
        weight = table[1].astype(f32) * (1.0 / 16.0)
        row, col = cell // COLS, cell % COLS
        ids, place = col_ids, col
        if first_col is not None:
            ids = edge_ids
            place = jnp.where((col >= first_col) & (col < first_col + 8), row % SPAN * 8 + col % 8, -1)
        for i in range(ROWS):
            at = slice(COLS * i, COLS * i + COLS)
            hot[:, at] = jnp.where(ids == place[i : i + 1, :], weight[i : i + 1, :], 0.0).astype(bf16)


def scatter_kernel(
    sums, left_table, own_table, right_table, col_hot, left_hot, right_hot,
    misfit, adj, to_pair, to_other,
    total, kept, lhs, edge_lhs,
):
    b = lax.axis_index("gy")
    acc = sums[0]
    for j in range(1, OWNERS):
        acc = acc + sums[j]
    total[...] = acc
    mine = acc[0:2]
    for d in range(1, OWNERS):
        mine = jnp.where(b == d, acc[2 * d : 2 * d + 2], mine)
    misfit[...] = mine
    sub = iota((8, COLS), 0)
    lane = iota((8, COLS), 1)
    tables = [
        [
            [
                jnp.where(
                    sub < 4,
                    jnp.broadcast_to(total[4 * q + c : 4 * q + c + 1, h : h + COLS], (8, COLS)),
                    jnp.broadcast_to(total[4 * q + 2 + c : 4 * q + 3 + c, h : h + COLS], (8, COLS)),
                )
                for h in (0, COLS)
            ]
            for c in range(2)
        ]
        for q in range(4)
    ]
    row_ids = iota((ROWS, COLS), 0)
    halo = [None, None, None]
    for k in (0, 2, 1):
        row = (left_table, own_table, right_table)[k][0] // COLS
        values = [[], []]
        for q in range(4):
            slot = (left_table, own_table, right_table)[k][2, 8 * q : 8 * q + 8, :]
            near = slot % COLS
            for c in range(2):
                values[c].append(
                    jnp.where(
                        slot < COLS,
                        jnp.take_along_axis(tables[q][c][0], near, axis=1),
                        jnp.take_along_axis(tables[q][c][1], near, axis=1),
                    )
                )
        parts = interleave(*(split3(jnp.concatenate(values[c], axis=0)) for c in range(2)))
        if k == 1:
            for i in range(ROWS):
                at = slice(COLS * i, COLS * i + COLS)
                hit = row_ids == row[i : i + 1, :]
                for p, part in enumerate(parts):
                    lhs[ROWS * p : ROWS * p + ROWS, at] = jnp.where(hit, part[i : i + 1, :], 0.0).astype(bf16)
            prod = contract_last(lhs[...], col_hot[...])
            for c in range(2):
                adj[c, :, 0:COLS] = sum(prod[ROWS * p : ROWS * p + ROWS] for p in (c, c + 2, c + 4))
        else:
            keep_parts(kept.at[k // 2], parts)
            group = row // SPAN
            for i in range(ROWS):
                block = parts_of_row(kept.at[k // 2], i)
                edge_lhs[:, COLS * i : COLS * i + COLS] = jnp.concatenate(
                    [jnp.where(group[i : i + 1, :] == g, block, 0.0) for g in range(ROWS // SPAN)], axis=0
                ).astype(bf16)
            prod = contract_last(edge_lhs[...], (right_hot if k else left_hot)[...])
            halo[k] = [sum_parts(prod[8 * g : 8 * g + 8]) for g in range(ROWS // SPAN)]
    for c in range(2):
        for q in range(4):
            first_row = 8 * q % SPAN
            where = ((first_row % 16 + sub) * 8 + lane % 8) % COLS
            sides = []
            for k in (2, 0):
                line = halo[k][8 * q // SPAN][c : c + 1]
                line = line[:, 8 * (first_row - first_row % 16) :][:, :COLS]
                if line.shape[1] < COLS:
                    line = jnp.concatenate([line, line], axis=1)
                sides.append(jnp.take_along_axis(jnp.broadcast_to(line, (8, COLS)), where, axis=1))
            adj[c, 8 * q : 8 * q + 8, COLS:] = jnp.where(lane < 8, sides[0], jnp.where(lane >= 120, sides[1], 0.0))
    to_pair[...], to_other[...] = facing_rows(adj[:, 0:8, :], adj[:, ROWS - 8 : ROWS, :])


def adjoint_kernel(adj, pair, other, window, rates, misfit, out, misfit_out, sem):
    copy = pltpu.make_async_copy(misfit, misfit_out, sem.at[0])
    copy.start()
    cover = window[0]
    visc = window[1]
    scaled = step_size * cover
    third = 0.25 * visc
    visc_p = prev_col(visc)
    third_p = 0.25 * visc_p
    states = []
    for c in range(2):
        above, below = above_below(pair, other, c)
        states.append(scaled * jnp.concatenate([above, adj[c], below], axis=0))
    w0, w1 = states
    own = slice(HALO, HALO + ROWS)
    a = h = t = h_p = t_p = None
    grad = None
    for step in range(SUBCYCLES - 2, -1, -1):
        w0_p, w1_p = prev_col(w0), prev_col(w1)
        ax = w0 - next_row(w0)
        ay = w1 - next_col(w1)
        at = (w0 - next_col(w0)) + (w1 - next_row(w1))
        ax_p = w0_p - next_row(w0_p)
        ay_p = w1_p - w1
        at_p = (w0_p - w0) + (w1_p - next_row(w1_p))
        da = 0.625 * ax + 0.375 * ay
        dh = 0.375 * ax + 0.625 * ay
        dh_p = 0.375 * ax_p + 0.625 * ay_p
        a = da if a is None else relax * a + da
        h = dh if h is None else relax * h + dh
        t = at if t is None else relax * t + at
        h_p = dh_p if h_p is None else relax * h_p + dh_p
        t_p = at_p if t_p is None else relax * t_p + at_p
        term = (
            a[own, :COLS] * rates[step, 0]
            + h[own, :COLS] * rates[step, 1]
            + 0.25 * (t[own, :COLS] * rates[step, 2])
        )
        grad = term if grad is None else grad + term
        if step:
            ra, rh, rt = visc * a, visc * h, third * t
            w0 = damping * w0 + scaled * ((prev_row(ra) - ra) + (third_p * t_p - rt))
            w1 = damping * w1 + scaled * ((visc_p * h_p - rh) + (prev_row(rt) - rt))
    grad = visc_scale * cover[own, :COLS] * grad
    rows = jnp.concatenate(
        [jnp.sum(grad[8 * i : 8 * i + 8], axis=0, keepdims=True) for i in range(ROWS // 8)], axis=0
    )
    gather = (iota((COLS, 16), 0) // 8 == iota((COLS, 16), 1)).astype(f32)
    parts = jnp.concatenate(split3(rows), axis=0).astype(bf16)
    sums = jnp.dot(parts, gather.astype(bf16), preferred_element_type=f32)
    out[...] = sums[0:4] + sums[4:8] + sums[8:12]
    copy.wait()


def call(kernel, outs, args, far=(), scratch=(), cost=0, limit=8):
    far = [pltpu.with_memory_space_constraint(x, pltpu.HBM) for x in far]
    near = pl.BlockSpec(memory_space=pltpu.VMEM)
    return pl.pallas_call(
        kernel,
        out_shape=tuple(outs),
        in_specs=[near] * len(args) + [pl.BlockSpec(memory_space=pltpu.HBM)] * len(far),
        out_specs=tuple(pl.BlockSpec(memory_space=o.memory_space) for o in outs),
        scratch_shapes=list(scratch),
        cost_estimate=pl.CostEstimate(flops=cost, bytes_accessed=0, transcendentals=0) if cost else None,
        compiler_params=pltpu.CompilerParams(vmem_limit_bytes=limit * 1024 * 1024),
    )(*args, *far)


def near(*shape, dtype=f32):
    return pltpu.VMEM(shape, dtype)


def per_device(forcing, strength, mask, send_cell, send_code, recv_buoy, observed):
    forcing = forcing[0]
    cells = send_cell.reshape(ROWS, COLS)
    codes = send_code.reshape(ROWS, COLS)
    recv = recv_buoy.reshape(ROWS, COLS)
    observed = observed.reshape(2, BUOYS)
    entries = ROWS * COLS
    packed, own, table, observed = call(
        pack_kernel,
        [near(OWNERS, 3, 4, COLS), near(4, ROWS, COLS), near(2, ROWS, COLS, dtype=jnp.int32), near(2, BUOYS)],
        (),
        (forcing, strength, mask, recv, cells, codes, observed),
        [
            near(2, ROWS, COLS),
            near(ROWS // 8, COLS // 8),
            near(ROWS, COLS, dtype=jnp.int32),
            near(ROWS, COLS, dtype=jnp.int32),
            pltpu.SemaphoreType.DMA((7,)),
        ],
    )
    received = lax.all_to_all(packed, "gy", 0, 0, tiled=True)
    ext, to_pair, to_other = call(
        widen_kernel,
        [near(4, ROWS, 2 * COLS), near(4, 8, 2 * COLS), near(4, 8, 2 * COLS)],
        (received, own),
    )
    pair, other = exchange_rows(to_pair, to_other)
    sums, rates, window, table = call(
        forward_kernel,
        [
            pltpu.HBM((OWNERS, 2 * OWNERS, BUOYS), f32),
            near(SUBCYCLES - 1, 3, ROWS, COLS),
            near(2, WIN, 2 * COLS),
            near(3, ROWS, COLS, dtype=jnp.int32),
        ],
        (ext, pair, other, received, table, observed),
        (),
        [
            near(2, ROWS, COLS),
            near(8 * ROWS, COLS),
            near(COLS, entries, dtype=bf16),
            near(2 * OWNERS, BUOYS),
            pltpu.SemaphoreType.DMA((OWNERS,)),
        ],
    )
    sums = lax.all_to_all(sums, "gy", 0, 0, tiled=True)
    left_table = from_behind(table, "gy", 1)
    right_table = from_behind(table, "gy", -1)
    col_hot, left_hot, right_hot = call(
        edge_kernel,
        [near(COLS, entries, dtype=bf16), near(8 * SPAN, entries, dtype=bf16), near(8 * SPAN, entries, dtype=bf16)],
        (table, left_table, right_table),
        cost=10**9,
    )
    misfit, adj, to_pair, to_other = call(
        scatter_kernel,
        [
            near(2, BUOYS),
            near(2, ROWS, 2 * COLS),
            near(2, 8, 2 * COLS),
            near(2, 8, 2 * COLS),
        ],
        (sums, left_table, table, right_table, col_hot, left_hot, right_hot),
        (),
        [
            near(2 * OWNERS, BUOYS),
            near(2, 8 * ROWS, COLS),
            near(6 * ROWS, entries, dtype=bf16),
            near(8 * ROWS // SPAN, entries, dtype=bf16),
        ],
    )
    pair, other = exchange_rows(to_pair, to_other)
    coarse, misfit = call(
        adjoint_kernel,
        [near(ROWS // 8, COLS // 8), pltpu.HBM((2, BUOYS), f32)],
        (adj, pair, other, window, rates, misfit),
        (),
        [pltpu.SemaphoreType.DMA((1,))],
    )
    gradient = jnp.sum(lax.all_gather(coarse, "member"), axis=0)
    return (misfit[None, None, None], gradient)


def solution(mesh):
    return jax.shard_map(
        per_device,
        mesh=mesh,
        in_specs=(
            P("member", None, "gx", "gy"),
            P("gx", "gy"),
            P("gx", "gy"),
            P("member", "gx", "gy", None),
            P("member", "gx", "gy", None),
            P("member", "gx", "gy", None),
            P("member", "gx", "gy", None, None),
        ),
        out_specs=(P("member", "gx", "gy", None, None), P("gx", "gy")),
        check_vma=False,
    )
```

```python
import jax
import jax.numpy as jnp
from jax import lax
from jax.experimental import pallas as pl
from jax.experimental.pallas import tpu as pltpu
from jax.sharding import PartitionSpec as P

SUBCYCLES = 8
BUOYS = 256
HALO = 8
ROWS = 32
COLS = 128
WIN = ROWS + 2 * HALO
OWNERS = 8
SPAN = 8

visc_scale = 0.2
relax = 0.6
step_size = 0.2
damping = 0.7

f32 = jnp.float32
bf16 = jnp.bfloat16


def from_behind(x, axis, by):
    count = lax.axis_size(axis)
    pairs = [(i, i + by) for i in range(count) if 0 <= i + by < count]
    return lax.ppermute(x, axis, pairs)


def facing_rows(first, last):
    even = lax.axis_index("gx") % 2 == 0
    return jnp.where(even, last, first), jnp.where(even, first, last)


def above_below(pair, other, f):
    a = lax.axis_index("gx")
    near = pair[1 - a % 2, f]
    far = other[f]
    even = a % 2 == 0
    return jnp.where(even, far, near), jnp.where(even, near, far)


def exchange_rows(to_pair, to_other):
    count = lax.axis_size("gx")
    swaps = [(i, i + 1) for i in range(1, count - 1, 2)]
    other = lax.ppermute(to_other, "gx", swaps + [(j, i) for i, j in swaps])
    groups = [[i, i + 1] for i in range(0, count, 2)]
    pair = lax.all_gather(to_pair, "gx", axis_index_groups=groups)
    return pair, other


def iota(shape, dim):
    return lax.broadcasted_iota(jnp.int32, shape, dim)


def split3(x):
    hi = x.astype(bf16).astype(f32)
    rest = x - hi
    mid = rest.astype(bf16).astype(f32)
    return hi, mid, rest - mid


def interleave(parts_u, parts_v):
    return [part for both in zip(parts_u, parts_v) for part in both]


def sum_parts(x):
    return x[0:2] + x[2:4] + x[4:6]


def contract_last(a, b):
    return lax.dot_general(a, b, (((1,), (1,)), ((), ())), preferred_element_type=f32)


def keep_parts(ref, parts):
    for p, part in enumerate(parts):
        ref[ROWS * p : ROWS * p + ROWS, :] = part
    ref[ROWS * len(parts) :, :] = jnp.zeros((ROWS * (8 - len(parts)), COLS), f32)


def parts_of_row(ref, i):
    return ref[pl.ds(i, 8, stride=ROWS), :]


def tile_fields(forcing, strength, mask):
    cover = mask.astype(f32)
    spread = (iota((16, COLS), 1) // 8 == iota((16, COLS), 0)).astype(f32)
    parts = jnp.concatenate(split3(strength), axis=0).astype(bf16)
    wide = jnp.dot(parts, spread.astype(bf16), preferred_element_type=f32)
    wide = (wide[0:4] + wide[4:8]) + wide[8:12]
    fine = jnp.concatenate([jnp.broadcast_to(wide[i : i + 1], (8, COLS)) for i in range(ROWS // 8)], axis=0)
    return forcing[0], forcing[1], cover, visc_scale * fine * cover


def pack_kernel(
    forcing_in, strength_in, mask_in, recv_in, cells_in, codes_in, observed_in,
    out, own, table, observed,
    forcing, strength, mask, recv, sems,
):
    b = lax.axis_index("gy")
    sources = (forcing_in, strength_in, mask_in, recv_in, cells_in, codes_in, observed_in)
    targets = (forcing, strength, mask, recv, table.at[0], table.at[1], observed)
    copies = [pltpu.make_async_copy(a, t, sems.at[i]) for i, (a, t) in enumerate(zip(sources, targets))]
    for copy in copies:
        copy.start()
    for copy in copies:
        copy.wait()
    fields = tile_fields(forcing[...], strength[...], mask[...])
    for f in range(4):
        own[f] = fields[f]
    lane = iota((8, COLS), 1)
    left = jnp.zeros((8, COLS), f32)
    right = jnp.zeros((8, COLS), f32)
    for g in range(4):
        for f in range(4):
            at = 32 * g + 8 * f
            piece = fields[f][8 * g : 8 * g + 8]
            here = (lane >= at) & (lane < at + 8)
            left = jnp.where(here, pltpu.roll(piece, at, 1) if at else piece, left)
            right = jnp.where(here, pltpu.roll(piece, at + 8, 1), right)
    slots = recv[...].astype(f32)
    for d in range(OWNERS):
        strip = jnp.where(d < b, left, right)
        out[d, 0] = strip[0:4]
        out[d, 1] = strip[4:8]
        out[d, 2] = slots[4 * d : 4 * d + 4]


def widen_kernel(received, own, ext, to_pair, to_other):
    b = lax.axis_index("gy")
    lane = iota((8, COLS), 1)
    left, right = jnp.maximum(b - 1, 0), jnp.minimum(b + 1, OWNERS - 1)
    from_left = jnp.concatenate([received[left, n] for n in range(2)], axis=0) * (b > 0).astype(f32)
    from_right = jnp.concatenate([received[right, n] for n in range(2)], axis=0) * (b < OWNERS - 1).astype(f32)
    for f in range(4):
        ext[f, :, 0:COLS] = own[f]
        for g in range(4):
            at = 32 * g + 8 * f
            low = pltpu.roll(from_right, (COLS - at) % COLS, 1) if at else from_right
            high = pltpu.roll(from_left, (120 - at) % COLS, 1)
            ext[f, 8 * g : 8 * g + 8, COLS:] = jnp.where(lane < 8, low, jnp.where(lane >= 120, high, 0.0))
    to_pair[...], to_other[...] = facing_rows(ext[:, 0:8, :], ext[:, ROWS - 8 : ROWS, :])


def next_row(x):
    return pltpu.roll(x, x.shape[0] - 1, 0)


def prev_row(x):
    return pltpu.roll(x, 1, 0)


def next_col(x):
    return pltpu.roll(x, x.shape[1] - 1, 1)


def prev_col(x):
    return pltpu.roll(x, 1, 1)


def forward_kernel(ext, pair, other, received, table, observed, sums, rates, window, table_out, vel, kept, hot, total, sems):
    b = lax.axis_index("gy")
    slot_ids = iota((COLS, COLS), 0)
    slots = jnp.concatenate([received[d, 2] for d in range(OWNERS)], axis=0).astype(jnp.int32)
    table_out[0] = table[0]
    table_out[1] = table[1]
    table_out[2] = slots
    for i in range(ROWS):
        at = slice(COLS * i, COLS * i + COLS)
        hot[:, at] = (slot_ids == slots[i : i + 1, :] % COLS).astype(f32).astype(bf16)
    fields = []
    for f in range(4):
        above, below = above_below(pair, other, f)
        fields.append(jnp.concatenate([above, ext[f], below], axis=0))
    force_x, force_y, cover, visc = fields
    window[0] = cover
    window[1] = visc
    tau_x = step_size * cover * force_x
    tau_y = step_size * cover * force_y
    big = (0.625 * step_size) * visc
    small = (0.375 * step_size) * visc
    quarter = (0.25 * step_size) * visc
    visc_p = prev_col(visc)
    big_p, small_p, quarter_p = ((c * step_size) * visc_p for c in (0.625, 0.375, 0.25))
    u, v = tau_x, tau_y
    nx = ny = s3 = ny_p = s3_p = None
    own = slice(HALO, HALO + ROWS)
    for step in range(SUBCYCLES - 1):
        u_p, v_p = prev_col(u), prev_col(v)
        ex = next_row(u) - u
        ey = next_col(v) - v
        sh = (next_col(u) - u) + (next_row(v) - v)
        ex_p = next_row(u_p) - u_p
        ey_p = v - v_p
        sh_p = (u - u_p) + (next_row(v_p) - v_p)
        rates[step, 0] = ex[own, :COLS]
        rates[step, 1] = ey[own, :COLS]
        rates[step, 2] = sh[own, :COLS]
        dx = big * ex + small * ey
        dy = small * ex + big * ey
        ds = quarter * sh
        dy_p = small_p * ex_p + big_p * ey_p
        ds_p = quarter_p * sh_p
        nx = dx if nx is None else relax * nx + dx
        ny = dy if ny is None else relax * ny + dy
        s3 = ds if s3 is None else relax * s3 + ds
        ny_p = dy_p if ny_p is None else relax * ny_p + dy_p
        s3_p = ds_p if s3_p is None else relax * s3_p + ds_p
        fx = (nx - prev_row(nx)) + (s3 - s3_p)
        fy = (ny - ny_p) + (s3 - prev_row(s3))
        u = damping * u + cover * fx + tau_x
        v = damping * v + cover * fy + tau_y
    vel[0] = u[own, :COLS]
    vel[1] = v[own, :COLS]

    cell = table[0]
    row, col = cell // COLS, cell % COLS
    got_u = jnp.zeros((ROWS, COLS), f32)
    got_v = jnp.zeros((ROWS, COLS), f32)
    for r in range(ROWS):
        hit = row == r
        line_u = jnp.broadcast_to(vel[0, r : r + 1, :], (ROWS, COLS))
        line_v = jnp.broadcast_to(vel[1, r : r + 1, :], (ROWS, COLS))
        got_u = jnp.where(hit, jnp.take_along_axis(line_u, col, axis=1), got_u)
        got_v = jnp.where(hit, jnp.take_along_axis(line_v, col, axis=1), got_v)
    weight = table[1].astype(f32) * (1.0 / 16.0)
    keep_parts(kept, interleave(split3(got_u * weight), split3(got_v * weight)))
    for d in range(OWNERS):
        left = []
        for i in range(4 * d, 4 * d + 4):
            block = parts_of_row(kept, i)
            low = slots[i : i + 1, :] < COLS
            left.append(jnp.concatenate([jnp.where(low, block, 0.0), jnp.where(low, 0.0, block)], axis=0))
        left = jnp.concatenate(left, axis=1).astype(bf16)
        prod = contract_last(left, hot[:, 4 * COLS * d : 4 * COLS * d + 4 * COLS])
        mine = (b == d).astype(f32)
        for h in range(2):
            at = slice(COLS * h, COLS * h + COLS)
            total[2 * d : 2 * d + 2, at] = sum_parts(prod[8 * h : 8 * h + 8]) - mine * observed[:, at]
    copies = [pltpu.make_async_copy(total, sums.at[d], sems.at[d]) for d in range(OWNERS)]
    for copy in copies:
        copy.start()
    for copy in copies:
        copy.wait()


def edge_kernel(own_table, left_table, right_table, col_hot, left_hot, right_hot):
    edge_ids = iota((8 * SPAN, COLS), 0)
    col_ids = iota((COLS, COLS), 0)
    for table, hot, first_col in ((own_table, col_hot, None), (left_table, left_hot, COLS - 8), (right_table, right_hot, 0)):
        cell = table[0]
        weight = table[1].astype(f32) * (1.0 / 16.0)
        row, col = cell // COLS, cell % COLS
        ids, place = col_ids, col
        if first_col is not None:
            ids = edge_ids
            place = jnp.where((col >= first_col) & (col < first_col + 8), row % SPAN * 8 + col % 8, -1)
        for i in range(ROWS):
            at = slice(COLS * i, COLS * i + COLS)
            hot[:, at] = jnp.where(ids == place[i : i + 1, :], weight[i : i + 1, :], 0.0).astype(bf16)


def scatter_kernel(
    sums, left_table, own_table, right_table, col_hot, left_hot, right_hot,
    misfit, adj, to_pair, to_other,
    total, kept, lhs, edge_lhs,
):
    b = lax.axis_index("gy")
    acc = sums[0]
    for j in range(1, OWNERS):
        acc = acc + sums[j]
    total[...] = acc
    mine = acc[0:2]
    for d in range(1, OWNERS):
        mine = jnp.where(b == d, acc[2 * d : 2 * d + 2], mine)
    misfit[...] = mine
    sub = iota((8, COLS), 0)
    lane = iota((8, COLS), 1)
    tables = [
        [
            [
                jnp.where(
                    sub < 4,
                    jnp.broadcast_to(total[4 * q + c : 4 * q + c + 1, h : h + COLS], (8, COLS)),
                    jnp.broadcast_to(total[4 * q + 2 + c : 4 * q + 3 + c, h : h + COLS], (8, COLS)),
                )
                for h in (0, COLS)
            ]
            for c in range(2)
        ]
        for q in range(4)
    ]
    row_ids = iota((ROWS, COLS), 0)
    halo = [None, None, None]
    for k in (0, 2, 1):
        row = (left_table, own_table, right_table)[k][0] // COLS
        values = [[], []]
        for q in range(4):
            slot = (left_table, own_table, right_table)[k][2, 8 * q : 8 * q + 8, :]
            near = slot % COLS
            for c in range(2):
                values[c].append(
                    jnp.where(
                        slot < COLS,
                        jnp.take_along_axis(tables[q][c][0], near, axis=1),
                        jnp.take_along_axis(tables[q][c][1], near, axis=1),
                    )
                )
        parts = interleave(*(split3(jnp.concatenate(values[c], axis=0)) for c in range(2)))
        if k == 1:
            for i in range(ROWS):
                at = slice(COLS * i, COLS * i + COLS)
                hit = row_ids == row[i : i + 1, :]
                for p, part in enumerate(parts):
                    lhs[ROWS * p : ROWS * p + ROWS, at] = jnp.where(hit, part[i : i + 1, :], 0.0).astype(bf16)
            prod = contract_last(lhs[...], col_hot[...])
            for c in range(2):
                adj[c, :, 0:COLS] = sum(prod[ROWS * p : ROWS * p + ROWS] for p in (c, c + 2, c + 4))
        else:
            keep_parts(kept.at[k // 2], parts)
            group = row // SPAN
            for i in range(ROWS):
                block = parts_of_row(kept.at[k // 2], i)
                edge_lhs[:, COLS * i : COLS * i + COLS] = jnp.concatenate(
                    [jnp.where(group[i : i + 1, :] == g, block, 0.0) for g in range(ROWS // SPAN)], axis=0
                ).astype(bf16)
            prod = contract_last(edge_lhs[...], (right_hot if k else left_hot)[...])
            halo[k] = [sum_parts(prod[8 * g : 8 * g + 8]) for g in range(ROWS // SPAN)]
    for c in range(2):
        for q in range(4):
            first_row = 8 * q % SPAN
            where = ((first_row % 16 + sub) * 8 + lane % 8) % COLS
            sides = []
            for k in (2, 0):
                line = halo[k][8 * q // SPAN][c : c + 1]
                line = line[:, 8 * (first_row - first_row % 16) :][:, :COLS]
                if line.shape[1] < COLS:
                    line = jnp.concatenate([line, line], axis=1)
                sides.append(jnp.take_along_axis(jnp.broadcast_to(line, (8, COLS)), where, axis=1))
            adj[c, 8 * q : 8 * q + 8, COLS:] = jnp.where(lane < 8, sides[0], jnp.where(lane >= 120, sides[1], 0.0))
    to_pair[...], to_other[...] = facing_rows(adj[:, 0:8, :], adj[:, ROWS - 8 : ROWS, :])


def adjoint_kernel(adj, pair, other, window, rates, misfit, out, misfit_out, sem):
    copy = pltpu.make_async_copy(misfit, misfit_out, sem.at[0])
    copy.start()
    cover = window[0]
    visc = window[1]
    scaled = step_size * cover
    third = 0.25 * visc
    visc_p = prev_col(visc)
    third_p = 0.25 * visc_p
    states = []
    for c in range(2):
        above, below = above_below(pair, other, c)
        states.append(scaled * jnp.concatenate([above, adj[c], below], axis=0))
    w0, w1 = states
    own = slice(HALO, HALO + ROWS)
    a = h = t = h_p = t_p = None
    grad = None
    for step in range(SUBCYCLES - 2, -1, -1):
        w0_p, w1_p = prev_col(w0), prev_col(w1)
        ax = w0 - next_row(w0)
        ay = w1 - next_col(w1)
        at = (w0 - next_col(w0)) + (w1 - next_row(w1))
        ax_p = w0_p - next_row(w0_p)
        ay_p = w1_p - w1
        at_p = (w0_p - w0) + (w1_p - next_row(w1_p))
        da = 0.625 * ax + 0.375 * ay
        dh = 0.375 * ax + 0.625 * ay
        dh_p = 0.375 * ax_p + 0.625 * ay_p
        a = da if a is None else relax * a + da
        h = dh if h is None else relax * h + dh
        t = at if t is None else relax * t + at
        h_p = dh_p if h_p is None else relax * h_p + dh_p
        t_p = at_p if t_p is None else relax * t_p + at_p
        term = (
            a[own, :COLS] * rates[step, 0]
            + h[own, :COLS] * rates[step, 1]
            + 0.25 * (t[own, :COLS] * rates[step, 2])
        )
        grad = term if grad is None else grad + term
        if step:
            ra, rh, rt = visc * a, visc * h, third * t
            w0 = damping * w0 + scaled * ((prev_row(ra) - ra) + (third_p * t_p - rt))
            w1 = damping * w1 + scaled * ((visc_p * h_p - rh) + (prev_row(rt) - rt))
    grad = visc_scale * cover[own, :COLS] * grad
    rows = jnp.concatenate(
        [jnp.sum(grad[8 * i : 8 * i + 8], axis=0, keepdims=True) for i in range(ROWS // 8)], axis=0
    )
    gather = (iota((COLS, 16), 0) // 8 == iota((COLS, 16), 1)).astype(f32)
    parts = jnp.concatenate(split3(rows), axis=0).astype(bf16)
    sums = jnp.dot(parts, gather.astype(bf16), preferred_element_type=f32)
    out[...] = sums[0:4] + sums[4:8] + sums[8:12]
    copy.wait()


def call(kernel, outs, args, far=(), scratch=(), cost=0, limit=8):
    far = [pltpu.with_memory_space_constraint(x, pltpu.HBM) for x in far]
    near = pl.BlockSpec(memory_space=pltpu.VMEM)
    return pl.pallas_call(
        kernel,
        out_shape=tuple(outs),
        in_specs=[near] * len(args) + [pl.BlockSpec(memory_space=pltpu.HBM)] * len(far),
        out_specs=tuple(pl.BlockSpec(memory_space=o.memory_space) for o in outs),
        scratch_shapes=list(scratch),
        cost_estimate=pl.CostEstimate(flops=cost, bytes_accessed=0, transcendentals=0) if cost else None,
        compiler_params=pltpu.CompilerParams(vmem_limit_bytes=limit * 1024 * 1024),
    )(*args, *far)


def near(*shape, dtype=f32):
    return pltpu.VMEM(shape, dtype)


def per_device(forcing, strength, mask, send_cell, send_code, recv_buoy, observed):
    forcing = forcing[0]
    cells = send_cell.reshape(ROWS, COLS)
    codes = send_code.reshape(ROWS, COLS)
    recv = recv_buoy.reshape(ROWS, COLS)
    observed = observed.reshape(2, BUOYS)
    entries = ROWS * COLS
    packed, own, table, observed = call(
        pack_kernel,
        [near(OWNERS, 3, 4, COLS), near(4, ROWS, COLS), near(2, ROWS, COLS, dtype=jnp.int32), near(2, BUOYS)],
        (),
        (forcing, strength, mask, recv, cells, codes, observed),
        [
            near(2, ROWS, COLS),
            near(ROWS // 8, COLS // 8),
            near(ROWS, COLS, dtype=jnp.int32),
            near(ROWS, COLS, dtype=jnp.int32),
            pltpu.SemaphoreType.DMA((7,)),
        ],
    )
    received = lax.all_to_all(packed, "gy", 0, 0, tiled=True)
    ext, to_pair, to_other = call(
        widen_kernel,
        [near(4, ROWS, 2 * COLS), near(4, 8, 2 * COLS), near(4, 8, 2 * COLS)],
        (received, own),
    )
    pair, other = exchange_rows(to_pair, to_other)
    sums, rates, window, table = call(
        forward_kernel,
        [
            pltpu.HBM((OWNERS, 2 * OWNERS, BUOYS), f32),
            near(SUBCYCLES - 1, 3, ROWS, COLS),
            near(2, WIN, 2 * COLS),
            near(3, ROWS, COLS, dtype=jnp.int32),
        ],
        (ext, pair, other, received, table, observed),
        (),
        [
            near(2, ROWS, COLS),
            near(8 * ROWS, COLS),
            near(COLS, entries, dtype=bf16),
            near(2 * OWNERS, BUOYS),
            pltpu.SemaphoreType.DMA((OWNERS,)),
        ],
    )
    sums = lax.all_to_all(sums, "gy", 0, 0, tiled=True)
    left_table = from_behind(table, "gy", 1)
    right_table = from_behind(table, "gy", -1)
    col_hot, left_hot, right_hot = call(
        edge_kernel,
        [near(COLS, entries, dtype=bf16), near(8 * SPAN, entries, dtype=bf16), near(8 * SPAN, entries, dtype=bf16)],
        (table, left_table, right_table),
        cost=10**9,
    )
    misfit, adj, to_pair, to_other = call(
        scatter_kernel,
        [
            near(2, BUOYS),
            near(2, ROWS, 2 * COLS),
            near(2, 8, 2 * COLS),
            near(2, 8, 2 * COLS),
        ],
        (sums, left_table, table, right_table, col_hot, left_hot, right_hot),
        (),
        [
            near(2 * OWNERS, BUOYS),
            near(2, 8 * ROWS, COLS),
            near(6 * ROWS, entries, dtype=bf16),
            near(8 * ROWS // SPAN, entries, dtype=bf16),
        ],
    )
    pair, other = exchange_rows(to_pair, to_other)
    coarse, misfit = call(
        adjoint_kernel,
        [near(ROWS // 8, COLS // 8), pltpu.HBM((2, BUOYS), f32)],
        (adj, pair, other, window, rates, misfit),
        (),
        [pltpu.SemaphoreType.DMA((1,))],
    )
    gradient = lax.psum(coarse, "member")
    return (misfit[None, None, None], gradient)


def solution(mesh):
    return jax.shard_map(
        per_device,
        mesh=mesh,
        in_specs=(
            P("member", None, "gx", "gy"),
            P("gx", "gy"),
            P("gx", "gy"),
            P("member", "gx", "gy", None),
            P("member", "gx", "gy", None),
            P("member", "gx", "gy", None),
            P("member", "gx", "gy", None, None),
        ),
        out_specs=(P("member", "gx", "gy", None, None), P("gx", "gy")),
        check_vma=False,
    )
```

```python
import jax
import jax.numpy as jnp
from jax import lax
from jax.experimental import pallas as pl
from jax.experimental.pallas import tpu as pltpu
from jax.sharding import PartitionSpec as P

SUBCYCLES = 8
BUOYS = 256
HALO = 8
ROWS = 32
COLS = 128
WIN = ROWS + 2 * HALO
OWNERS = 8
SPAN = 8

visc_scale = 0.2
relax = 0.6
step_size = 0.2
damping = 0.7

f32 = jnp.float32
bf16 = jnp.bfloat16


def from_behind(x, axis, by):
    count = lax.axis_size(axis)
    pairs = [(i, i + by) for i in range(count) if 0 <= i + by < count]
    return lax.ppermute(x, axis, pairs)


def facing_rows(first, last):
    even = lax.axis_index("gx") % 2 == 0
    return jnp.where(even, last, first), jnp.where(even, first, last)


def above_below(pair, other, f):
    a = lax.axis_index("gx")
    near = pair[1 - a % 2, f]
    far = other[f]
    even = a % 2 == 0
    return jnp.where(even, far, near), jnp.where(even, near, far)


def exchange_rows(to_pair, to_other):
    count = lax.axis_size("gx")
    swaps = [(i, i + 1) for i in range(1, count - 1, 2)]
    other = lax.ppermute(to_other, "gx", swaps + [(j, i) for i, j in swaps])
    groups = [[i, i + 1] for i in range(0, count, 2)]
    pair = lax.all_gather(to_pair, "gx", axis_index_groups=groups)
    return pair, other


def iota(shape, dim):
    return lax.broadcasted_iota(jnp.int32, shape, dim)


def split3(x):
    hi = x.astype(bf16).astype(f32)
    rest = x - hi
    mid = rest.astype(bf16).astype(f32)
    return hi, mid, rest - mid


def interleave(parts_u, parts_v):
    return [part for both in zip(parts_u, parts_v) for part in both]


def sum_parts(x):
    return x[0:2] + x[2:4] + x[4:6]


def contract_last(a, b):
    return lax.dot_general(a, b, (((1,), (1,)), ((), ())), preferred_element_type=f32)


def keep_parts(ref, parts):
    for p, part in enumerate(parts):
        ref[ROWS * p : ROWS * p + ROWS, :] = part
    ref[ROWS * len(parts) :, :] = jnp.zeros((ROWS * (8 - len(parts)), COLS), f32)


def parts_of_row(ref, i):
    return ref[pl.ds(i, 8, stride=ROWS), :]


def tile_fields(forcing, strength, mask):
    cover = mask.astype(f32)
    cells_y = COLS // 8
    padded = jnp.concatenate([strength, jnp.zeros((ROWS // 8, COLS - cells_y), f32)], axis=1)
    padded = jnp.concatenate([padded, padded], axis=0)
    wide = jnp.take_along_axis(padded, iota((8, COLS), 1) // 8, axis=1)
    fine = jnp.concatenate([jnp.broadcast_to(wide[i : i + 1], (8, COLS)) for i in range(ROWS // 8)], axis=0)
    return forcing[0], forcing[1], cover, visc_scale * fine * cover


def pack_kernel(
    forcing_in, strength_in, mask_in, recv_in, cells_in, codes_in, observed_in,
    out, own, table, observed,
    forcing, strength, mask, recv, sems,
):
    b = lax.axis_index("gy")
    sources = (forcing_in, strength_in, mask_in, recv_in, cells_in, codes_in, observed_in)
    targets = (forcing, strength, mask, recv, table.at[0], table.at[1], observed)
    copies = [pltpu.make_async_copy(a, t, sems.at[i]) for i, (a, t) in enumerate(zip(sources, targets))]
    for copy in copies:
        copy.start()
    for copy in copies[:3]:
        copy.wait()
    fields = tile_fields(forcing[...], strength[...], mask[...])
    for f in range(4):
        own[f] = fields[f]
    lane = iota((8, COLS), 1)
    left = jnp.zeros((8, COLS), f32)
    right = jnp.zeros((8, COLS), f32)
    for g in range(4):
        for f in range(4):
            at = 32 * g + 8 * f
            piece = fields[f][8 * g : 8 * g + 8]
            here = (lane >= at) & (lane < at + 8)
            left = jnp.where(here, pltpu.roll(piece, at, 1) if at else piece, left)
            right = jnp.where(here, pltpu.roll(piece, at + 8, 1), right)
    for copy in copies[3:]:
        copy.wait()
    slots = recv[...].astype(f32)
    for d in range(OWNERS):
        strip = jnp.where(d < b, left, right)
        out[d, 0] = strip[0:4]
        out[d, 1] = strip[4:8]
        out[d, 2] = slots[4 * d : 4 * d + 4]


def widen_kernel(received, own, ext, to_pair, to_other):
    b = lax.axis_index("gy")
    lane = iota((8, COLS), 1)
    left, right = jnp.maximum(b - 1, 0), jnp.minimum(b + 1, OWNERS - 1)
    from_left = jnp.concatenate([received[left, n] for n in range(2)], axis=0) * (b > 0).astype(f32)
    from_right = jnp.concatenate([received[right, n] for n in range(2)], axis=0) * (b < OWNERS - 1).astype(f32)
    for f in range(4):
        ext[f, :, 0:COLS] = own[f]
        for g in range(4):
            at = 32 * g + 8 * f
            low = pltpu.roll(from_right, (COLS - at) % COLS, 1) if at else from_right
            high = pltpu.roll(from_left, (120 - at) % COLS, 1)
            ext[f, 8 * g : 8 * g + 8, COLS:] = jnp.where(lane < 8, low, jnp.where(lane >= 120, high, 0.0))
    to_pair[...], to_other[...] = facing_rows(ext[:, 0:8, :], ext[:, ROWS - 8 : ROWS, :])


def next_row(x):
    return pltpu.roll(x, x.shape[0] - 1, 0)


def prev_row(x):
    return pltpu.roll(x, 1, 0)


def next_col(x):
    return pltpu.roll(x, x.shape[1] - 1, 1)


def prev_col(x):
    return pltpu.roll(x, 1, 1)


def slot_kernel(received, table, table_out, hot):
    slot_ids = iota((COLS, COLS), 0)
    slots = jnp.concatenate([received[d, 2] for d in range(OWNERS)], axis=0).astype(jnp.int32)
    table_out[0] = table[0]
    table_out[1] = table[1]
    table_out[2] = slots
    for i in range(ROWS):
        at = slice(COLS * i, COLS * i + COLS)
        hot[:, at] = (slot_ids == slots[i : i + 1, :] % COLS).astype(f32).astype(bf16)


def forward_kernel(ext, pair, other, table, hot, observed, sums, rates, window, vel, kept, total, sems):
    b = lax.axis_index("gy")
    fields = []
    for f in range(4):
        above, below = above_below(pair, other, f)
        fields.append(jnp.concatenate([above, ext[f], below], axis=0))
    force_x, force_y, cover, visc = fields
    window[0] = cover
    window[1] = visc
    tau_x = step_size * cover * force_x
    tau_y = step_size * cover * force_y
    big = (0.625 * step_size) * visc
    small = (0.375 * step_size) * visc
    quarter = (0.25 * step_size) * visc
    visc_p = prev_col(visc)
    big_p, small_p, quarter_p = ((c * step_size) * visc_p for c in (0.625, 0.375, 0.25))
    u, v = tau_x, tau_y
    nx = ny = s3 = ny_p = s3_p = None
    own = slice(HALO, HALO + ROWS)
    for step in range(SUBCYCLES - 1):
        u_p, v_p = prev_col(u), prev_col(v)
        ex = next_row(u) - u
        ey = next_col(v) - v
        sh = (next_col(u) - u) + (next_row(v) - v)
        ex_p = next_row(u_p) - u_p
        ey_p = v - v_p
        sh_p = (u - u_p) + (next_row(v_p) - v_p)
        rates[step, 0] = ex[own, :COLS]
        rates[step, 1] = ey[own, :COLS]
        rates[step, 2] = sh[own, :COLS]
        dx = big * ex + small * ey
        dy = small * ex + big * ey
        ds = quarter * sh
        dy_p = small_p * ex_p + big_p * ey_p
        ds_p = quarter_p * sh_p
        nx = dx if nx is None else relax * nx + dx
        ny = dy if ny is None else relax * ny + dy
        s3 = ds if s3 is None else relax * s3 + ds
        ny_p = dy_p if ny_p is None else relax * ny_p + dy_p
        s3_p = ds_p if s3_p is None else relax * s3_p + ds_p
        fx = (nx - prev_row(nx)) + (s3 - s3_p)
        fy = (ny - ny_p) + (s3 - prev_row(s3))
        u = damping * u + cover * fx + tau_x
        v = damping * v + cover * fy + tau_y
    vel[0] = u[own, :COLS]
    vel[1] = v[own, :COLS]

    cell = table[0]
    slots = table[2]
    row, col = cell // COLS, cell % COLS
    got_u = jnp.zeros((ROWS, COLS), f32)
    got_v = jnp.zeros((ROWS, COLS), f32)
    for r in range(ROWS):
        hit = row == r
        line_u = jnp.broadcast_to(vel[0, r : r + 1, :], (ROWS, COLS))
        line_v = jnp.broadcast_to(vel[1, r : r + 1, :], (ROWS, COLS))
        got_u = jnp.where(hit, jnp.take_along_axis(line_u, col, axis=1), got_u)
        got_v = jnp.where(hit, jnp.take_along_axis(line_v, col, axis=1), got_v)
    weight = table[1].astype(f32) * (1.0 / 16.0)
    keep_parts(kept, interleave(split3(got_u * weight), split3(got_v * weight)))
    for d in range(OWNERS):
        left = []
        for i in range(4 * d, 4 * d + 4):
            block = parts_of_row(kept, i)
            low = slots[i : i + 1, :] < COLS
            left.append(jnp.concatenate([jnp.where(low, block, 0.0), jnp.where(low, 0.0, block)], axis=0))
        left = jnp.concatenate(left, axis=1).astype(bf16)
        prod = contract_last(left, hot[:, 4 * COLS * d : 4 * COLS * d + 4 * COLS])
        mine = (b == d).astype(f32)
        for h in range(2):
            at = slice(COLS * h, COLS * h + COLS)
            total[2 * d : 2 * d + 2, at] = sum_parts(prod[8 * h : 8 * h + 8]) - mine * observed[:, at]
    copies = [pltpu.make_async_copy(total, sums.at[d], sems.at[d]) for d in range(OWNERS)]
    for copy in copies:
        copy.start()
    for copy in copies:
        copy.wait()


def edge_kernel(own_table, left_table, right_table, col_hot, left_hot, right_hot):
    edge_ids = iota((8 * SPAN, COLS), 0)
    col_ids = iota((COLS, COLS), 0)
    for table, hot, first_col in ((own_table, col_hot, None), (left_table, left_hot, COLS - 8), (right_table, right_hot, 0)):
        cell = table[0]
        weight = table[1].astype(f32) * (1.0 / 16.0)
        row, col = cell // COLS, cell % COLS
        ids, place = col_ids, col
        if first_col is not None:
            ids = edge_ids
            place = jnp.where((col >= first_col) & (col < first_col + 8), row % SPAN * 8 + col % 8, -1)
        for i in range(ROWS):
            at = slice(COLS * i, COLS * i + COLS)
            hot[:, at] = jnp.where(ids == place[i : i + 1, :], weight[i : i + 1, :], 0.0).astype(bf16)


def scatter_kernel(
    sums, left_table, own_table, right_table, col_hot, left_hot, right_hot,
    misfit, adj, to_pair, to_other,
    total, kept, lhs, edge_lhs,
):
    b = lax.axis_index("gy")
    acc = sums[0]
    for j in range(1, OWNERS):
        acc = acc + sums[j]
    total[...] = acc
    mine = acc[0:2]
    for d in range(1, OWNERS):
        mine = jnp.where(b == d, acc[2 * d : 2 * d + 2], mine)
    misfit[...] = mine
    sub = iota((8, COLS), 0)
    lane = iota((8, COLS), 1)
    tables = [
        [
            [
                jnp.where(
                    sub < 4,
                    jnp.broadcast_to(total[4 * q + c : 4 * q + c + 1, h : h + COLS], (8, COLS)),
                    jnp.broadcast_to(total[4 * q + 2 + c : 4 * q + 3 + c, h : h + COLS], (8, COLS)),
                )
                for h in (0, COLS)
            ]
            for c in range(2)
        ]
        for q in range(4)
    ]
    row_ids = iota((ROWS, COLS), 0)
    halo = [None, None, None]
    for k in (0, 2, 1):
        row = (left_table, own_table, right_table)[k][0] // COLS
        values = [[], []]
        for q in range(4):
            slot = (left_table, own_table, right_table)[k][2, 8 * q : 8 * q + 8, :]
            near = slot % COLS
            for c in range(2):
                values[c].append(
                    jnp.where(
                        slot < COLS,
                        jnp.take_along_axis(tables[q][c][0], near, axis=1),
                        jnp.take_along_axis(tables[q][c][1], near, axis=1),
                    )
                )
        parts = interleave(*(split3(jnp.concatenate(values[c], axis=0)) for c in range(2)))
        if k == 1:
            for i in range(ROWS):
                at = slice(COLS * i, COLS * i + COLS)
                hit = row_ids == row[i : i + 1, :]
                for p, part in enumerate(parts):
                    lhs[ROWS * p : ROWS * p + ROWS, at] = jnp.where(hit, part[i : i + 1, :], 0.0).astype(bf16)
            prod = contract_last(lhs[...], col_hot[...])
            for c in range(2):
                adj[c, :, 0:COLS] = sum(prod[ROWS * p : ROWS * p + ROWS] for p in (c, c + 2, c + 4))
        else:
            keep_parts(kept.at[k // 2], parts)
            group = row // SPAN
            for i in range(ROWS):
                block = parts_of_row(kept.at[k // 2], i)
                edge_lhs[:, COLS * i : COLS * i + COLS] = jnp.concatenate(
                    [jnp.where(group[i : i + 1, :] == g, block, 0.0) for g in range(ROWS // SPAN)], axis=0
                ).astype(bf16)
            prod = contract_last(edge_lhs[...], (right_hot if k else left_hot)[...])
            halo[k] = [sum_parts(prod[8 * g : 8 * g + 8]) for g in range(ROWS // SPAN)]
    for c in range(2):
        for q in range(4):
            first_row = 8 * q % SPAN
            where = ((first_row % 16 + sub) * 8 + lane % 8) % COLS
            sides = []
            for k in (2, 0):
                line = halo[k][8 * q // SPAN][c : c + 1]
                line = line[:, 8 * (first_row - first_row % 16) :][:, :COLS]
                if line.shape[1] < COLS:
                    line = jnp.concatenate([line, line], axis=1)
                sides.append(jnp.take_along_axis(jnp.broadcast_to(line, (8, COLS)), where, axis=1))
            adj[c, 8 * q : 8 * q + 8, COLS:] = jnp.where(lane < 8, sides[0], jnp.where(lane >= 120, sides[1], 0.0))
    to_pair[...], to_other[...] = facing_rows(adj[:, 0:8, :], adj[:, ROWS - 8 : ROWS, :])


def adjoint_kernel(adj, pair, other, window, rates, misfit, out, misfit_out, sem):
    copy = pltpu.make_async_copy(misfit, misfit_out, sem.at[0])
    copy.start()
    cover = window[0]
    visc = window[1]
    scaled = step_size * cover
    third = 0.25 * visc
    visc_p = prev_col(visc)
    third_p = 0.25 * visc_p
    states = []
    for c in range(2):
        above, below = above_below(pair, other, c)
        states.append(scaled * jnp.concatenate([above, adj[c], below], axis=0))
    w0, w1 = states
    own = slice(HALO, HALO + ROWS)
    a = h = t = h_p = t_p = None
    grad = None
    for step in range(SUBCYCLES - 2, -1, -1):
        w0_p, w1_p = prev_col(w0), prev_col(w1)
        ax = w0 - next_row(w0)
        ay = w1 - next_col(w1)
        at = (w0 - next_col(w0)) + (w1 - next_row(w1))
        ax_p = w0_p - next_row(w0_p)
        ay_p = w1_p - w1
        at_p = (w0_p - w0) + (w1_p - next_row(w1_p))
        da = 0.625 * ax + 0.375 * ay
        dh = 0.375 * ax + 0.625 * ay
        dh_p = 0.375 * ax_p + 0.625 * ay_p
        a = da if a is None else relax * a + da
        h = dh if h is None else relax * h + dh
        t = at if t is None else relax * t + at
        h_p = dh_p if h_p is None else relax * h_p + dh_p
        t_p = at_p if t_p is None else relax * t_p + at_p
        term = (
            a[own, :COLS] * rates[step, 0]
            + h[own, :COLS] * rates[step, 1]
            + 0.25 * (t[own, :COLS] * rates[step, 2])
        )
        grad = term if grad is None else grad + term
        if step:
            ra, rh, rt = visc * a, visc * h, third * t
            w0 = damping * w0 + scaled * ((prev_row(ra) - ra) + (third_p * t_p - rt))
            w1 = damping * w1 + scaled * ((visc_p * h_p - rh) + (prev_row(rt) - rt))
    grad = visc_scale * cover[own, :COLS] * grad
    rows = jnp.concatenate(
        [jnp.sum(grad[8 * i : 8 * i + 8], axis=0, keepdims=True) for i in range(ROWS // 8)], axis=0
    )
    gather = (iota((COLS, 16), 0) // 8 == iota((COLS, 16), 1)).astype(f32)
    parts = jnp.concatenate(split3(rows), axis=0).astype(bf16)
    sums = jnp.dot(parts, gather.astype(bf16), preferred_element_type=f32)
    out[...] = sums[0:4] + sums[4:8] + sums[8:12]
    copy.wait()


def call(kernel, outs, args, far=(), scratch=(), cost=0, limit=8):
    far = [pltpu.with_memory_space_constraint(x, pltpu.HBM) for x in far]
    near = pl.BlockSpec(memory_space=pltpu.VMEM)
    return pl.pallas_call(
        kernel,
        out_shape=tuple(outs),
        in_specs=[near] * len(args) + [pl.BlockSpec(memory_space=pltpu.HBM)] * len(far),
        out_specs=tuple(pl.BlockSpec(memory_space=o.memory_space) for o in outs),
        scratch_shapes=list(scratch),
        cost_estimate=pl.CostEstimate(flops=cost, bytes_accessed=0, transcendentals=0) if cost else None,
        compiler_params=pltpu.CompilerParams(vmem_limit_bytes=limit * 1024 * 1024),
    )(*args, *far)


def near(*shape, dtype=f32):
    return pltpu.VMEM(shape, dtype)


def per_device(forcing, strength, mask, send_cell, send_code, recv_buoy, observed):
    forcing = forcing[0]
    cells = send_cell.reshape(ROWS, COLS)
    codes = send_code.reshape(ROWS, COLS)
    recv = recv_buoy.reshape(ROWS, COLS)
    observed = observed.reshape(2, BUOYS)
    entries = ROWS * COLS
    packed, own, table, observed = call(
        pack_kernel,
        [near(OWNERS, 3, 4, COLS), near(4, ROWS, COLS), near(2, ROWS, COLS, dtype=jnp.int32), near(2, BUOYS)],
        (),
        (forcing, strength, mask, recv, cells, codes, observed),
        [
            near(2, ROWS, COLS),
            near(ROWS // 8, COLS // 8),
            near(ROWS, COLS, dtype=jnp.int32),
            near(ROWS, COLS, dtype=jnp.int32),
            pltpu.SemaphoreType.DMA((7,)),
        ],
    )
    received = lax.all_to_all(packed, "gy", 0, 0, tiled=True)
    ext, to_pair, to_other = call(
        widen_kernel,
        [near(4, ROWS, 2 * COLS), near(4, 8, 2 * COLS), near(4, 8, 2 * COLS)],
        (received, own),
    )
    pair, other = exchange_rows(to_pair, to_other)
    table, slot_hot = call(
        slot_kernel,
        [near(3, ROWS, COLS, dtype=jnp.int32), near(COLS, entries, dtype=bf16)],
        (received, table),
        cost=10**9,
    )
    sums, rates, window = call(
        forward_kernel,
        [
            pltpu.HBM((OWNERS, 2 * OWNERS, BUOYS), f32),
            near(SUBCYCLES - 1, 3, ROWS, COLS),
            near(2, WIN, 2 * COLS),
        ],
        (ext, pair, other, table, slot_hot, observed),
        (),
        [near(2, ROWS, COLS), near(8 * ROWS, COLS), near(2 * OWNERS, BUOYS), pltpu.SemaphoreType.DMA((OWNERS,))],
    )
    sums = lax.all_to_all(sums, "gy", 0, 0, tiled=True)
    left_table = from_behind(table, "gy", 1)
    right_table = from_behind(table, "gy", -1)
    col_hot, left_hot, right_hot = call(
        edge_kernel,
        [near(COLS, entries, dtype=bf16), near(8 * SPAN, entries, dtype=bf16), near(8 * SPAN, entries, dtype=bf16)],
        (table, left_table, right_table),
        cost=10**9,
    )
    misfit, adj, to_pair, to_other = call(
        scatter_kernel,
        [
            near(2, BUOYS),
            near(2, ROWS, 2 * COLS),
            near(2, 8, 2 * COLS),
            near(2, 8, 2 * COLS),
        ],
        (sums, left_table, table, right_table, col_hot, left_hot, right_hot),
        (),
        [
            near(2 * OWNERS, BUOYS),
            near(2, 8 * ROWS, COLS),
            near(6 * ROWS, entries, dtype=bf16),
            near(8 * ROWS // SPAN, entries, dtype=bf16),
        ],
    )
    pair, other = exchange_rows(to_pair, to_other)
    coarse, misfit = call(
        adjoint_kernel,
        [near(ROWS // 8, COLS // 8), pltpu.HBM((2, BUOYS), f32)],
        (adj, pair, other, window, rates, misfit),
        (),
        [pltpu.SemaphoreType.DMA((1,))],
    )
    gradient = jnp.sum(lax.all_gather(coarse, "member"), axis=0)
    return (misfit[None, None, None], gradient)


def solution(mesh):
    return jax.shard_map(
        per_device,
        mesh=mesh,
        in_specs=(
            P("member", None, "gx", "gy"),
            P("gx", "gy"),
            P("gx", "gy"),
            P("member", "gx", "gy", None),
            P("member", "gx", "gy", None),
            P("member", "gx", "gy", None),
            P("member", "gx", "gy", None, None),
        ),
        out_specs=(P("member", "gx", "gy", None, None), P("gx", "gy")),
        check_vma=False,
    )
```
